32 devices in a mesh: groups: 2 (over x), rows: 16 (over z, y, core).
Axes of the slice: x: 2, y: 2, z: 4, core: 2. Of those that a mesh axis runs over, the one named last changes fastest.
Arguments:
- sequence_features: bfloat16 [2048, 32, 64], P(('groups', 'rows')), parts along dimension 0
- sequence_presence: int32 [2048, 32], P(('groups', 'rows')), parts along dimension 0, may hold values from 0 to 1, as said below
- position_presence: int32 [64], P('groups'), parts along dimension 0, may hold values from 0 to 1, as said below
- product_scale_vector: float32 [64], replicated, may hold values from 0.1 to 1.9
- product_shift_vector: float32 [64], replicated, may hold values from -3 to 3
- first_factor_matrix: bfloat16 [64, 32], replicated, may hold values from -0.75 to 0.75
- second_factor_matrix: bfloat16 [64, 32], replicated, may hold values from -0.75 to 0.75
- coupling_matrix: bfloat16 [1024, 128], replicated, may hold values from -0.1875 to 0.1875
- coupling_offset: float32 [128], replicated, may hold values from -3 to 3
- feedforward_scale_vector: float32 [64], replicated, may hold values from 0.1 to 1.9
- feedforward_shift_vector: float32 [64], replicated, may hold values from -3 to 3
- feedforward_switch_matrix: bfloat16 [64, 256], replicated, may hold values from -0.75 to 0.75
- feedforward_expand_matrix: bfloat16 [64, 256], replicated, may hold values from -0.75 to 0.75
- feedforward_contract_matrix: bfloat16 [256, 64], replicated, may hold values from -0.375 to 0.375
Outputs:
- pair_mean_update: float32 [2048, 128], P(('groups', 'rows')), parts along dimension 0
- refreshed_sequences: bfloat16 [2048, 32, 64], P(('groups', 'rows')), parts along dimension 0
The draws below stay inside these ranges and needn't reach their ends.
There are 2 independent parts, one for each index of `groups`. The reference program is written for one: setup_inputs(seed, part) draws one part's arguments, and reference() takes and returns one part's arrays. A program takes and returns all parts, laid end to end along the dimension named above; an argument that names none is the same for every part. Nothing has to cross between parts.
Inputs may be any that keep to these rules, and one draw needn't show every extreme that they name: `sequence_presence`: 0 or 1; rows further down the MSA are less often valid. `position_presence`: 0 or 1; the last residue is invalid.
All inputs are finite; a program needn't handle non-finite values.
Results may differ from the reference program's by a relative error of at most 0.0046.
Values sent between devices are 32-bit elements; how exact they have to be, the bound alone decides.
No kernel may reach another device: no remote copies, remote signals or barrier semaphores. Data moves between devices by JAX's collectives and lax.ppermute only.
A program may use at most 128 MiB of HBM per device.

```python
import jax
import jax.numpy as jnp
from jax import lax

C = 64
H = 32
CZ = 128
N = 32
S = 1024
HH = 1024
FOURC = 256


def draw_sequence_features(key, part):
    key = jax.random.fold_in(key, 11)
    key_base, key_noise = jax.random.split(key)
    base = jax.random.normal(key_base, (N, C), jnp.float32)
    noise = jax.random.normal(key_noise, (S, N, C), jnp.float32)
    return (base[None, :, :] + noise).astype(jnp.bfloat16)


def draw_sequence_presence(key, part):
    key = jax.random.fold_in(key, 12)
    drawn = jax.random.randint(key, (S, N), 0, 1000)
    level = 950 - 650 * jnp.arange(S, dtype=jnp.int32) // S
    return (drawn < level[:, None]).astype(jnp.int32)


def draw_position_presence(key, part):
    key = jax.random.fold_in(key, 13)
    key_length, key_holes = jax.random.split(key)
    length = jax.random.randint(key_length, (), N - N // 4, N)
    holes = jax.random.randint(key_holes, (N,), 0, 10)
    kept = (jnp.arange(N, dtype=jnp.int32) < length) & (holes != 0)
    return kept.astype(jnp.int32)


def scatter_about(key, dims, spread, limit, kind=jnp.bfloat16):
    result = jax.random.normal(key, dims, jnp.float32) * spread
    return jnp.minimum(jnp.maximum(result, -limit), limit).astype(kind)


def setup_inputs(seed: int = 0, part: int = 0) -> dict:
    splits = jax.random.split(jax.random.key(seed), 15)
    own_keys = jax.random.split(jax.random.fold_in(splits[14], part), 15)
    sequence_features = draw_sequence_features(jax.random.fold_in(jax.random.fold_in(splits[14], part), 71), part)
    sequence_presence = draw_sequence_presence(jax.random.fold_in(jax.random.fold_in(splits[14], part), 71), part)
    position_presence = draw_position_presence(jax.random.fold_in(jax.random.fold_in(splits[14], part), 71), part)
    product_scale_vector = jnp.clip(1.0 + 0.18 * jax.random.normal(splits[3], (C,), jnp.float32), 0.1, 1.9)
    product_shift_vector = scatter_about(splits[4], (C,), 0.5, 3.0, jnp.float32)
    first_factor_matrix = scatter_about(splits[5], (C, H), C ** -0.5, 0.75)
    second_factor_matrix = scatter_about(splits[6], (C, H), C ** -0.5, 0.75)
    coupling_matrix = scatter_about(splits[7], (HH, CZ), HH ** -0.5, 0.1875)
    coupling_offset = scatter_about(splits[8], (CZ,), 0.5, 3.0, jnp.float32)
    feedforward_scale_vector = jnp.clip(1.0 + 0.18 * jax.random.normal(splits[9], (C,), jnp.float32), 0.1, 1.9)
    feedforward_shift_vector = scatter_about(splits[10], (C,), 0.5, 3.0, jnp.float32)
    feedforward_switch_matrix = scatter_about(splits[11], (C, FOURC), C ** -0.5, 0.75)
    feedforward_expand_matrix = scatter_about(splits[12], (C, FOURC), C ** -0.5, 0.75)
    feedforward_contract_matrix = scatter_about(splits[13], (FOURC, C), FOURC ** -0.5, 0.375)
    return {"sequence_features": sequence_features, "sequence_presence": sequence_presence, "position_presence": position_presence, "product_scale_vector": product_scale_vector, "product_shift_vector": product_shift_vector, "first_factor_matrix": first_factor_matrix, "second_factor_matrix": second_factor_matrix, "coupling_matrix": coupling_matrix, "coupling_offset": coupling_offset, "feedforward_scale_vector": feedforward_scale_vector, "feedforward_shift_vector": feedforward_shift_vector, "feedforward_switch_matrix": feedforward_switch_matrix, "feedforward_expand_matrix": feedforward_expand_matrix, "feedforward_contract_matrix": feedforward_contract_matrix}


def standardize_features(values, gain, bias):
    values = values.astype(jnp.float32)
    mean = lax.optimization_barrier(jnp.mean(values, axis=-1, keepdims=True))
    centered = values - mean
    variance = lax.optimization_barrier(jnp.mean(centered * centered, axis=-1, keepdims=True))
    return centered / jnp.sqrt(variance + 1e-05) * gain + bias

def reference(sequence_features, sequence_presence, position_presence, product_scale_vector, product_shift_vector, first_factor_matrix, second_factor_matrix, coupling_matrix, coupling_offset, feedforward_scale_vector, feedforward_shift_vector, feedforward_switch_matrix, feedforward_expand_matrix, feedforward_contract_matrix):
    valid_flags = (sequence_presence * position_presence[None, :]).astype(jnp.float32)
    standardized_lines = standardize_features(sequence_features, product_scale_vector, product_shift_vector).astype(jnp.bfloat16)
    left = (jnp.dot(standardized_lines, first_factor_matrix, preferred_element_type=jnp.float32) * valid_flags[:, :, None]).astype(jnp.bfloat16)
    right = (jnp.dot(standardized_lines, second_factor_matrix, preferred_element_type=jnp.float32) * valid_flags[:, :, None]).astype(jnp.bfloat16)
    left_flat = left.astype(jnp.float32).reshape(S, N * H)
    right_flat = right.astype(jnp.float32).reshape(S, N * H)
    outer = jnp.dot(left_flat.T, right_flat, precision=lax.Precision.HIGHEST)
    outer = outer.reshape(N, H, N, H).transpose(0, 2, 1, 3).reshape(N * N, H * H)
    counts = jnp.dot(valid_flags.T, valid_flags, precision=lax.Precision.HIGHEST).reshape(N * N)
    projected = jnp.dot(outer, coupling_matrix.astype(jnp.float32), precision=lax.Precision.HIGHEST)
    pair_mean_update = projected / jnp.maximum(counts, 1.0)[:, None] + coupling_offset
    feedforward_standardized = standardize_features(sequence_features, feedforward_scale_vector, feedforward_shift_vector).astype(jnp.bfloat16)
    gate = jnp.dot(feedforward_standardized, feedforward_switch_matrix, preferred_element_type=jnp.float32)
    upper = jnp.dot(feedforward_standardized, feedforward_expand_matrix, preferred_element_type=jnp.float32)
    feedforward_inner = (jax.nn.silu(gate) * upper).astype(jnp.bfloat16)
    refreshed_sequences = (sequence_features.astype(jnp.float32) + jnp.dot(feedforward_inner, feedforward_contract_matrix, preferred_element_type=jnp.float32)).astype(jnp.bfloat16)
    return (pair_mean_update, refreshed_sequences)
```

```python
import functools

import jax
import jax.numpy as jnp
from jax import lax
from jax.experimental import pallas as pl
from jax.experimental.pallas import tpu as pltpu
from jax.sharding import PartitionSpec as P

F32 = jnp.float32
BF16 = jnp.bfloat16
EPS = 1e-05
LANES = 128


def dot(a, b, dims=((1,), (0,))):
    return lax.dot_general(a, b, (dims, ((), ())), preferred_element_type=F32)


def two_halves(array, half):
    return jnp.concatenate([array[:, :half, :], array[:, half:, :]], axis=-1)


def twice(vector):
    return jnp.concatenate([vector, vector], axis=-1)


def block_pair(matrix):
    zero = jnp.zeros_like(matrix)
    return jnp.concatenate(
        [jnp.concatenate([matrix, zero], axis=1), jnp.concatenate([zero, matrix], axis=1)], axis=0
    )


def mean_matrix(channels):
    row = lax.broadcasted_iota(jnp.int32, (2 * channels, 2 * channels), 0) // channels
    column = lax.broadcasted_iota(jnp.int32, (2 * channels, 2 * channels), 1) // channels
    return jnp.where(row == column, 1.0 / channels, 0.0).astype(BF16)


def standardize_pairs(values, averaging, gain, bias):
    wide = values.astype(F32)
    centered = wide - dot(values, averaging)
    variance = dot((centered * centered).astype(BF16), averaging)
    return centered * lax.rsqrt(variance + EPS) * gain + bias


def outer_kernel(
    x_hbm, presence_hbm, position_hbm, gain_hbm, bias_hbm, first_hbm, second_hbm, coupling_hbm,
    out_ref,
    x_ref, presence_ref, position_ref, gain_ref, bias_ref, first_ref, second_ref, coupling_ref, arrived,
    x_scratch, left_t_scratch, left_scratch, x_mat,
):
    copies = [
        pltpu.make_async_copy(source, target, arrived.at[n])
        for n, (source, target) in enumerate((
            (x_hbm, x_ref),
            (presence_hbm, presence_ref),
            (position_hbm, position_ref),
            (gain_hbm, gain_ref),
            (bias_hbm, bias_ref),
            (first_hbm, first_ref),
            (second_hbm, second_ref),
            (coupling_hbm, coupling_ref),
        ))
    ]
    for copy in copies:
        copy.start()
    rows, residues, channels = x_ref.shape
    hidden = first_ref.shape[0]
    half = residues // 2
    quad = LANES // hidden
    groups = hidden // quad

    for copy in copies[:-1]:
        copy.wait()
    x_scratch[...] = two_halves(x_ref[...], half).astype(F32).reshape(rows * half, 2 * channels)
    tokens = jnp.concatenate(
        [x_scratch[pl.ds(p, rows, stride=half), :] for p in range(half)], axis=0
    ).astype(BF16)
    normed = standardize_pairs(tokens, mean_matrix(channels), twice(gain_ref[...]), twice(bias_ref[...]))

    square = (residues, residues)
    diagonal = lax.broadcasted_iota(jnp.int32, square, 0) == lax.broadcasted_iota(jnp.int32, square, 1)
    position = jnp.where(diagonal, position_ref[...].astype(F32), 0.0).sum(axis=1, keepdims=True)
    valid = (presence_ref[...].astype(F32) * position).astype(BF16)
    spread_row = lax.broadcasted_iota(jnp.int32, (residues, half * 2 * channels), 0)
    spread_column = lax.broadcasted_iota(jnp.int32, (residues, half * 2 * channels), 1)
    wanted = spread_column // (2 * channels) + half * ((spread_column % (2 * channels)) // channels)
    spread = jnp.where(spread_row == wanted, 1.0, 0.0).astype(BF16)
    flags = dot(valid, spread, ((0,), (0,)))
    flags = jnp.concatenate(
        [flags[:, p * 2 * channels : (p + 1) * 2 * channels] for p in range(half)], axis=0
    )
    normed = (normed * flags).astype(BF16)

    left_t = dot(block_pair(first_ref[...]), normed, ((1,), (1,)))
    for v in range(left_t_scratch.shape[0]):
        left_t_scratch[v] = left_t[:, v * LANES : (v + 1) * LANES]
    low = lax.broadcasted_iota(jnp.int32, (groups, LANES), 1) < rows
    per = LANES // rows
    for side in range(2):
        for v in range(half // per):
            pieces = [
                left_t_scratch[v, pl.ds(side * hidden + h4, groups, stride=quad), :]
                for h4 in range(quad)
            ]
            turned = [pltpu.roll(piece, rows, 1) for piece in pieces]
            for odd in range(2):
                residue = side * half + v * per + odd
                for c in range(quad // 2):
                    if odd:
                        tile = jnp.where(low, turned[2 * c], pieces[2 * c + 1])
                    else:
                        tile = jnp.where(low, pieces[2 * c], turned[2 * c + 1])
                    left_scratch[c, pl.ds(residue, groups, stride=residues), :] = tile
    left = jnp.concatenate(
        [left_scratch[c] for c in range(quad // 2)], axis=1
    ).astype(BF16)

    second = second_ref[...]
    repeated = jnp.concatenate([second] * quad, axis=0)
    right = dot(normed, block_pair(repeated), ((1,), (1,))).astype(BF16)
    lane_group = lax.broadcasted_iota(jnp.int32, (rows, LANES), 1) // hidden
    masks = [lane_group == h4 for h4 in range(quad)]
    zero = jnp.zeros((rows, LANES), BF16)
    for j in range(residues):
        side, p = j // half, j % half
        one = right[p * rows : (p + 1) * rows, side * LANES : (side + 1) * LANES]
        spread_right = jnp.concatenate([jnp.where(m, one, zero) for m in masks], axis=0)
        product = dot(left, spread_right).astype(BF16)
        for g in range(groups):
            x_mat[j * residues : (j + 1) * residues, g * LANES : (g + 1) * LANES] = product[
                g * residues : (g + 1) * residues, :
            ]
    copies[-1].wait()
    projected = dot(x_mat[...], coupling_ref[...])
    for j in range(residues - 1):
        out_ref[pl.ds(j, residues, stride=residues), :] = projected[j * residues : (j + 1) * residues, :]
    counts = dot(valid, valid, ((1,), (1,)))
    out_ref[pl.ds(residues - 1, residues, stride=residues), :] = jnp.concatenate(
        [counts, jnp.zeros((residues, LANES - residues), F32)], axis=1
    )


def transition_kernel(x_ref, gain_ref, bias_ref, switch_ref, expand_ref, contract_ref, out_ref):
    rows, residues, channels = x_ref.shape
    half = residues // 2
    averaging = mean_matrix(channels)
    gain, bias = twice(gain_ref[...]), twice(bias_ref[...])
    switch = block_pair(switch_ref[...])
    expand = block_pair(expand_ref[...])
    contract = block_pair(contract_ref[...])
    step = 16
    for start in range(0, rows, step):
        pairs = two_halves(x_ref[start : start + step], half).reshape(step * half, 2 * channels)
        normed = standardize_pairs(pairs, averaging, gain, bias).astype(BF16)
        gate = dot(normed, switch) * 0.5
        inner = ((gate + gate * jnp.tanh(gate)) * dot(normed, expand)).astype(BF16)
        result = (pairs.astype(F32) + dot(inner, contract, ((1,), (1,)))).astype(BF16)
        result = result.reshape(step, half, 2 * channels)
        out_ref[start : start + step, :half, :] = result[:, :, :channels]
        out_ref[start : start + step, half:, :] = result[:, :, channels:]


def pick(array, index, axis):
    return lax.dynamic_index_in_dim(array, index, axis, keepdims=False)


def scatter_sum(partial, size):
    me = lax.axis_index("rows")
    tail = partial.shape[1:]
    done = 1
    while size // done > 4 or (size // done) % 4:
        left = size // done
        parts = partial.reshape((left // 2, 2) + tail)
        mine = (me // done) % 2
        partner = [(i, i ^ done) for i in range(size)]
        partial = pick(parts, mine, 1) + lax.ppermute(pick(parts, 1 - mine, 1), "rows", partner)
        done *= 2
    mine = me // done
    total = pick(partial, mine, 0)
    for k in range(1, size // done):
        partner = [(i, i ^ (k * done)) for i in range(size)]
        total = total + lax.ppermute(pick(partial, mine ^ k, 0), "rows", partner)
    return total


def body(
    sequence_features,
    sequence_presence,
    position_presence,
    product_scale_vector,
    product_shift_vector,
    first_factor_matrix,
    second_factor_matrix,
    coupling_matrix,
    coupling_offset,
    feedforward_scale_vector,
    feedforward_shift_vector,
    feedforward_switch_matrix,
    feedforward_expand_matrix,
    feedforward_contract_matrix,
    *,
    size,
):
    rows, residues, channels = sequence_features.shape
    hidden = first_factor_matrix.shape[1]
    pair_channels = coupling_matrix.shape[1]
    pairs = residues * residues
    row = lambda v: v.reshape(1, -1)
    operands = (
        sequence_features,
        sequence_presence.T,
        row(position_presence),
        row(product_scale_vector),
        row(product_shift_vector),
        first_factor_matrix.T,
        second_factor_matrix.T,
        coupling_matrix,
    )
    partial = pl.pallas_call(
        outer_kernel,
        out_shape=jax.ShapeDtypeStruct((pairs, pair_channels), F32),
        in_specs=[pl.BlockSpec(memory_space=pltpu.HBM)] * len(operands),
        out_specs=pl.BlockSpec(memory_space=pltpu.VMEM),
        scratch_shapes=[pltpu.VMEM(operand.shape, operand.dtype) for operand in operands] + [
            pltpu.SemaphoreType.DMA((len(operands),)),
            pltpu.VMEM((rows * residues // 2, 2 * channels), F32),
            pltpu.VMEM((rows * residues // 2 // LANES, 2 * hidden, LANES), F32),
            pltpu.VMEM((rows // hidden, pairs * hidden // LANES, LANES), F32),
            pltpu.VMEM((pairs, hidden * hidden), BF16),
        ],
        compiler_params=pltpu.CompilerParams(vmem_limit_bytes=48 * 1024 * 1024),
        name="outer_products",
    )(*(pltpu.with_memory_space_constraint(operand, pltpu.HBM) for operand in operands))
    refreshed_sequences = pl.pallas_call(
        transition_kernel,
        out_shape=jax.ShapeDtypeStruct(sequence_features.shape, BF16),
        compiler_params=pltpu.CompilerParams(vmem_limit_bytes=48 * 1024 * 1024),
        cost_estimate=pl.CostEstimate(flops=400_000_000, bytes_accessed=2_000_000, transcendentals=600_000),
        name="transition",
    )(
        sequence_features,
        row(feedforward_scale_vector),
        row(feedforward_shift_vector),
        feedforward_switch_matrix,
        feedforward_expand_matrix,
        feedforward_contract_matrix.T,
    )
    own = pairs // size
    if own % residues == 0:
        summed = scatter_sum(partial.reshape(size, own, pair_channels), size)
        summed = summed.reshape(own // residues, residues, pair_channels)
        counted = summed[:, residues - 1, :residues, None]
        last = lax.broadcasted_iota(jnp.int32, summed.shape, 1) == residues - 1
        summed = jnp.where(last, 0.0, summed)
        pair_mean_update = summed / jnp.maximum(counted, 1.0) + coupling_offset
    else:
        grid = partial.reshape(residues, residues, pair_channels)
        counted = lax.psum(grid[:, residues - 1, :residues], "rows").reshape(size, own)
        counted = pick(counted, lax.axis_index("rows"), 0)[:, None]
        last = lax.broadcasted_iota(jnp.int32, grid.shape, 1) == residues - 1
        summed = scatter_sum(jnp.where(last, 0.0, grid).reshape(size, own, pair_channels), size)
        pair_mean_update = summed / jnp.maximum(counted, 1.0) + coupling_offset
    return pair_mean_update.reshape(own, pair_channels), refreshed_sequences


def solution(mesh):
    everywhere = P()
    in_specs = (
        P(("groups", "rows"), None, None),
        P(("groups", "rows"), None),
        P("groups"),
    ) + (everywhere,) * 11
    out_specs = (P(("groups", "rows"), None), P(("groups", "rows"), None, None))
    return jax.shard_map(
        functools.partial(body, size=mesh.shape["rows"]),
        mesh=mesh, in_specs=in_specs, out_specs=out_specs, check_vma=False,
    )
```

```python
import functools

import jax
import jax.numpy as jnp
from jax import lax
from jax.experimental import pallas as pl
from jax.experimental.pallas import tpu as pltpu
from jax.sharding import PartitionSpec as P

F32 = jnp.float32
BF16 = jnp.bfloat16
EPS = 1e-05
LANES = 128
VMEM_LIMIT = 48 * 1024 * 1024
STEP = 16
OWNERS = 16


def dot(a, b, dims=((1,), (0,))):
    return lax.dot_general(a, b, (dims, ((), ())), preferred_element_type=F32)


def two_halves(array, half):
    return jnp.concatenate([array[:, :half, :], array[:, half:, :]], axis=-1)


def twice(vector):
    return jnp.concatenate([vector, vector], axis=-1)


def block_pair(matrix):
    zero = jnp.zeros_like(matrix)
    return jnp.concatenate(
        [jnp.concatenate([matrix, zero], axis=1), jnp.concatenate([zero, matrix], axis=1)], axis=0
    )


def iota(shape, axis):
    return lax.broadcasted_iota(jnp.int32, shape, axis)


def mean_matrix(channels):
    shape = (2 * channels, 2 * channels)
    same = iota(shape, 0) // channels == iota(shape, 1) // channels
    return jnp.where(same, 1.0 / channels, 0.0).astype(BF16)


def standardize_pairs(values, averaging, gain, bias):
    centered = values.astype(F32) - dot(values, averaging)
    variance = dot((centered * centered).astype(BF16), averaging)
    return centered * lax.rsqrt(variance + EPS) * gain + bias


def place(residue, me, per_owner):
    if me is None:
        return residue
    apart = (residue // per_owner) ^ me
    rank = (apart & 1) * 8 + ((apart >> 1) & 1) * 4 + ((apart >> 2) ^ 2)
    return rank * per_owner + residue % per_owner


def outer_kernel(relative, n_inputs, n_handed, *refs):
    sources = refs[:n_inputs]
    keep_ref, send_ref = refs[n_inputs : n_inputs + 2]
    handed = refs[n_inputs + 2 : n_inputs + 2 + n_handed]
    own = n_inputs - n_handed
    targets = refs[n_inputs + 2 + n_handed :][:own]
    arrived, x_scratch, left_t_scratch, left_scratch, x_mat = refs[n_inputs + 2 + n_handed + own :]
    presence_ref, position_ref, gain_ref, bias_ref, first_ref, second_ref, coupling_ref = targets
    x_ref = handed[0]
    me = lax.axis_index("rows") if relative else None
    order = (handed[0],) + tuple(targets) + tuple(handed[1:])
    copies = [
        pltpu.make_async_copy(source, target, arrived.at[n])
        for n, (source, target) in enumerate(zip(sources, order))
    ]
    for copy in copies:
        copy.start()
    rows, residues, channels = x_ref.shape
    hidden = first_ref.shape[0]
    half = residues // 2
    per_owner = residues // OWNERS
    quad = LANES // hidden
    groups = hidden // quad
    square = (residues, residues)

    for copy in copies[:own]:
        copy.wait()
    x_scratch[...] = two_halves(x_ref[...], half).astype(F32).reshape(rows * half, 2 * channels)
    tokens = jnp.concatenate(
        [x_scratch[pl.ds(p, rows, stride=half), :] for p in range(half)], axis=0
    ).astype(BF16)
    normed = standardize_pairs(tokens, mean_matrix(channels), twice(gain_ref[...]), twice(bias_ref[...]))

    diagonal = iota(square, 0) == iota(square, 1)
    position = jnp.where(diagonal, position_ref[...].astype(F32), 0.0).sum(axis=1, keepdims=True)
    valid = (presence_ref[...].astype(F32) * position).astype(BF16)
    lanes = iota((residues, half * 2 * channels), 1)
    wanted = lanes // (2 * channels) + half * ((lanes % (2 * channels)) // channels)
    spread = jnp.where(iota(lanes.shape, 0) == wanted, 1.0, 0.0).astype(BF16)
    flags = dot(valid, spread, ((0,), (0,)))
    flags = jnp.concatenate(
        [flags[:, p * 2 * channels : (p + 1) * 2 * channels] for p in range(half)], axis=0
    )
    normed = (normed * flags).astype(BF16)

    left_t = dot(block_pair(first_ref[...]), normed, ((1,), (1,)))
    for v in range(left_t_scratch.shape[0]):
        left_t_scratch[v] = left_t[:, v * LANES : (v + 1) * LANES]
    low = iota((groups, LANES), 1) < rows
    per = LANES // rows
    for side in range(2):
        for v in range(half // per):
            pieces = [
                left_t_scratch[v, pl.ds(side * hidden + h4, groups, stride=quad), :]
                for h4 in range(quad)
            ]
            turned = [pltpu.roll(piece, rows, 1) for piece in pieces]
            for odd in range(2):
                row = place(side * half + v * per + odd, me, per_owner)
                for c in range(quad // 2):
                    if odd:
                        tile = jnp.where(low, turned[2 * c], pieces[2 * c + 1])
                    else:
                        tile = jnp.where(low, pieces[2 * c], turned[2 * c + 1])
                    left_scratch[c, pl.ds(row, groups, stride=residues), :] = tile
    left = jnp.concatenate(
        [left_scratch[c] for c in range(quad // 2)], axis=1
    ).astype(BF16)

    repeated = jnp.concatenate([second_ref[...]] * quad, axis=0)
    right = dot(normed, block_pair(repeated), ((1,), (1,))).astype(BF16)
    lane_group = iota((rows, LANES), 1) // hidden
    masks = [lane_group == h4 for h4 in range(quad)]
    zero = jnp.zeros((rows, LANES), BF16)
    for j in range(residues):
        side, p = j // half, j % half
        one = right[p * rows : (p + 1) * rows, side * LANES : (side + 1) * LANES]
        spread_right = jnp.concatenate([jnp.where(m, one, zero) for m in masks], axis=0)
        product = dot(left, spread_right).astype(BF16)
        for g in range(groups):
            x_mat[j * residues : (j + 1) * residues, g * LANES : (g + 1) * LANES] = product[
                g * residues : (g + 1) * residues, :
            ]
    copies[own].wait()
    projected = dot(x_mat[...], coupling_ref[...])
    order = (place(iota(square, 1), me, per_owner) == iota(square, 0)).astype(BF16)
    counts = dot(dot(order, valid).astype(BF16), valid, ((1,), (1,)))
    counts = jnp.concatenate([counts, jnp.zeros((residues, LANES - residues), F32)], axis=1)
    for j in range(residues):
        rows_j = counts if j == residues - 1 else projected[j * residues : (j + 1) * residues, :]
        keep_ref[pl.ds(j, half, stride=residues), :] = rows_j[:half]
        send_ref[pl.ds(j, half, stride=residues), :] = rows_j[half:]
    for copy in copies[own + 1 :]:
        copy.wait()


def transition_rows(x_ref, start, count, gain_ref, bias_ref, switch_ref, expand_ref, contract_ref, out_ref):
    _, residues, channels = x_ref.shape
    half = residues // 2
    averaging = mean_matrix(channels)
    gain, bias = twice(gain_ref[...]), twice(bias_ref[...])
    switch = block_pair(switch_ref[...])
    expand = block_pair(expand_ref[...])
    contract = block_pair(contract_ref[...])
    for at in range(0, count, STEP):
        pairs = two_halves(x_ref[start + at : start + at + STEP], half).reshape(STEP * half, 2 * channels)
        normed = standardize_pairs(pairs, averaging, gain, bias).astype(BF16)
        gate = dot(normed, switch) * 0.5
        inner = ((gate + gate * jnp.tanh(gate)) * dot(normed, expand)).astype(BF16)
        result = (pairs.astype(F32) + dot(inner, contract, ((1,), (1,)))).astype(BF16)
        result = result.reshape(STEP, half, 2 * channels)
        out_ref[at : at + STEP, :half, :] = result[:, :, :channels]
        out_ref[at : at + STEP, half:, :] = result[:, :, channels:]
        yield at


def transition_head(x_ref, *refs):
    *weight_refs, out_ref = refs
    for _ in transition_rows(x_ref, 0, out_ref.shape[0], *weight_refs, out_ref):
        pass


def transition_tail(x_ref, *refs):
    *weight_refs, head_ref, out_hbm, result_ref, sent = refs
    head = head_ref.shape[0]
    copies = [pltpu.make_async_copy(head_ref, out_hbm.at[pl.ds(0, head)], sent.at[0])]
    copies[0].start()
    for at in transition_rows(x_ref, head, result_ref.shape[0], *weight_refs, result_ref):
        copies.append(
            pltpu.make_async_copy(
                result_ref.at[pl.ds(at, STEP)], out_hbm.at[pl.ds(head + at, STEP)], sent.at[len(copies)]
            )
        )
        copies[-1].start()
    for copy in copies:
        copy.wait()


def finish_kernel(residues, *refs):
    *summand_refs, offset_ref, out_ref = refs
    total = summand_refs[0][...]
    for ref in summand_refs[1:]:
        total = total + ref[...]
    square = (residues, residues)
    diagonal = iota(square, 0) == iota(square, 1)
    last = iota((residues, total.shape[1]), 0) == residues - 1
    for start in range(0, total.shape[0], residues):
        block = total[start : start + residues]
        counts = jnp.where(diagonal, block[residues - 1 :, :residues], 0.0).sum(axis=1, keepdims=True)
        mean = jnp.where(last, 0.0, block) / jnp.maximum(counts, 1.0)
        out_ref[start : start + residues, :] = mean + offset_ref[...]


def pick(array, index, axis):
    return lax.dynamic_index_in_dim(array, index, axis, keepdims=False)


def swap(array, size, apart):
    return lax.ppermute(array, "rows", [(i, i ^ apart) for i in range(size)])


def scatter_sum(partial, size):
    me = lax.axis_index("rows")
    tail = partial.shape[1:]
    done = 1
    while size // done > 4 or (size // done) % 4:
        parts = partial.reshape((size // done // 2, 2) + tail)
        mine = (me // done) % 2
        partial = pick(parts, mine, 1) + swap(pick(parts, 1 - mine, 1), size, done)
        done *= 2
    mine = me // done
    total = pick(partial, mine, 0)
    for k in range(1, size // done):
        total = total + swap(pick(partial, mine ^ k, 0), size, k * done)
    return total


def inside(shape, dtype):
    return pltpu.VMEM(shape, dtype)


def transition(features, weights, head_rows):
    rows, residues, channels = features.shape
    vmem = pl.BlockSpec(memory_space=pltpu.VMEM)
    cost = lambda count: pl.CostEstimate(
        flops=6_000_000 * count, bytes_accessed=30_000 * count, transcendentals=8_000 * count
    )
    params = pltpu.CompilerParams(vmem_limit_bytes=VMEM_LIMIT)
    pinned = [pltpu.with_memory_space_constraint(a, pltpu.VMEM) for a in (features,) + tuple(weights)]
    head = lambda: pl.pallas_call(
        transition_head,
        out_shape=inside((head_rows, residues, channels), BF16),
        in_specs=[vmem] * len(pinned),
        out_specs=vmem,
        compiler_params=params,
        cost_estimate=cost(head_rows),
        name="transition_head",
    )(*pinned)
    tail = lambda before: pl.pallas_call(
        transition_tail,
        out_shape=jax.ShapeDtypeStruct(features.shape, BF16),
        in_specs=[vmem] * (len(pinned) + 1),
        out_specs=pl.BlockSpec(memory_space=pltpu.HBM),
        scratch_shapes=[
            pltpu.VMEM((rows - head_rows, residues, channels), BF16),
            pltpu.SemaphoreType.DMA((1 + (rows - head_rows) // STEP,)),
        ],
        compiler_params=params,
        cost_estimate=cost(rows - head_rows),
        name="transition_tail",
    )(*pinned, pltpu.with_memory_space_constraint(before, pltpu.VMEM))
    return head, tail


def body(
    sequence_features,
    sequence_presence,
    position_presence,
    product_scale_vector,
    product_shift_vector,
    first_factor_matrix,
    second_factor_matrix,
    coupling_matrix,
    coupling_offset,
    feedforward_scale_vector,
    feedforward_shift_vector,
    feedforward_switch_matrix,
    feedforward_expand_matrix,
    feedforward_contract_matrix,
    *,
    size,
):
    rows, residues, channels = sequence_features.shape
    hidden = first_factor_matrix.shape[1]
    pair_channels = coupling_matrix.shape[1]
    pairs = residues * residues
    own = pairs // size
    relative = size == OWNERS
    row = lambda v: v.reshape(1, -1)
    used = (
        sequence_presence.T,
        row(position_presence),
        row(product_scale_vector),
        row(product_shift_vector),
        first_factor_matrix.T,
        second_factor_matrix.T,
        coupling_matrix,
    )
    handed = (
        sequence_features,
        row(coupling_offset),
        row(feedforward_scale_vector),
        row(feedforward_shift_vector),
        feedforward_switch_matrix,
        feedforward_expand_matrix,
        feedforward_contract_matrix.T,
    )
    operands = handed[:1] + used + handed[1:]
    results = [inside((pairs // 2, pair_channels), F32)] * 2
    results += [inside(operand.shape, operand.dtype) for operand in handed]
    keep, send, features, offset, *weights = pl.pallas_call(
        functools.partial(outer_kernel, relative, len(operands), len(handed)),
        out_shape=results,
        in_specs=[pl.BlockSpec(memory_space=pltpu.HBM)] * len(operands),
        out_specs=[pl.BlockSpec(memory_space=pltpu.VMEM)] * len(results),
        scratch_shapes=[pltpu.VMEM(operand.shape, operand.dtype) for operand in used] + [
            pltpu.SemaphoreType.DMA((len(operands),)),
            pltpu.VMEM((rows * residues // 2, 2 * channels), F32),
            pltpu.VMEM((rows * residues // 2 // LANES, 2 * hidden, LANES), F32),
            pltpu.VMEM((rows // hidden, pairs * hidden // LANES, LANES), F32),
            pltpu.VMEM((pairs, hidden * hidden), BF16),
        ],
        compiler_params=pltpu.CompilerParams(vmem_limit_bytes=VMEM_LIMIT),
        name="outer_products",
    )(*(pltpu.with_memory_space_constraint(operand, pltpu.HBM) for operand in operands))
    head, tail = transition(features, weights, rows // 4)
    if relative:
        keep = keep.reshape(2, 4, own, pair_channels)
        head_rows = head()
        got, head_rows = lax.optimization_barrier((swap(send, size, 1), head_rows))
        got = got.reshape(2, 4, own, pair_channels)
        away = keep[1] + got[1]
        far = swap(away[:2], size, 2)
        near = swap(away[2:], size, 2)
        here = keep[0] + got[0]
        upper = here[:2] + far
        two, three = swap(upper[0], size, 8), swap(upper[1], size, 12)
        lower = here[2:] + near
        one = swap(lower[1], size, 4)
        refreshed = tail(head_rows)
        summands = (two, three, one, lower[0])
        pair_mean_update = pl.pallas_call(
            functools.partial(finish_kernel, residues),
            out_shape=jax.ShapeDtypeStruct((own, pair_channels), F32),
            in_specs=[pl.BlockSpec(memory_space=pltpu.VMEM)] * (len(summands) + 1),
            compiler_params=pltpu.CompilerParams(vmem_limit_bytes=VMEM_LIMIT),
            name="finish",
        )(*(pltpu.with_memory_space_constraint(a, pltpu.VMEM) for a in summands + (offset,)))
    else:
        refreshed = tail(head())
        grid = jnp.concatenate([keep.reshape(residues // 2, residues, pair_channels),
                                send.reshape(residues // 2, residues, pair_channels)], axis=0)
        counted = lax.psum(grid[:, residues - 1, :residues], "rows").reshape(size, own)
        counted = pick(counted, lax.axis_index("rows"), 0)[:, None]
        last = iota(grid.shape, 1) == residues - 1
        summed = scatter_sum(jnp.where(last, 0.0, grid).reshape(size, own, pair_channels), size)
        pair_mean_update = summed / jnp.maximum(counted, 1.0) + coupling_offset
    return pair_mean_update, refreshed


def solution(mesh):
    in_specs = (
        P(("groups", "rows"), None, None),
        P(("groups", "rows"), None),
        P("groups"),
    ) + (P(),) * 11
    out_specs = (P(("groups", "rows"), None), P(("groups", "rows"), None, None))
    return jax.shard_map(
        functools.partial(body, size=mesh.shape["rows"]),
        mesh=mesh, in_specs=in_specs, out_specs=out_specs, check_vma=False,
    )
```

```python
import functools

import jax
import jax.numpy as jnp
from jax import lax
from jax.experimental import pallas as pl
from jax.experimental.pallas import tpu as pltpu
from jax.sharding import PartitionSpec as P

F32 = jnp.float32
BF16 = jnp.bfloat16
EPS = 1e-05
LANES = 128
VMEM_LIMIT = 48 * 1024 * 1024
STEP = 16
JOIN = 2
CHUNK = 512
FIRST_HOP = (2, 3, 1, 0)
SECOND_HOP = (3, 2, 0, 1)
OWNERS = 16


def dot(a, b, dims=((1,), (0,))):
    return lax.dot_general(a, b, (dims, ((), ())), preferred_element_type=F32)


def two_halves(array, half):
    return jnp.concatenate([array[:, :half, :], array[:, half:, :]], axis=-1)


def twice(vector):
    return jnp.concatenate([vector, vector], axis=-1)


def block_pair(matrix):
    zero = jnp.zeros_like(matrix)
    return jnp.concatenate(
        [jnp.concatenate([matrix, zero], axis=1), jnp.concatenate([zero, matrix], axis=1)], axis=0
    )


def iota(shape, axis):
    return lax.broadcasted_iota(jnp.int32, shape, axis)


def mean_matrix(channels):
    shape = (2 * channels, 2 * channels)
    same = iota(shape, 0) // channels == iota(shape, 1) // channels
    return jnp.where(same, 1.0 / channels, 0.0).astype(BF16)


def standardize_pairs(values, averaging, gain, bias):
    centered = values.astype(F32) - dot(values, averaging)
    variance = dot((centered * centered).astype(BF16), averaging)
    return centered * lax.rsqrt(variance + EPS) * gain + bias


def place(residue, me, per_owner):
    if me is None:
        return residue
    apart = (residue // per_owner) ^ me
    along = apart >> 2
    swapped = (along >> 1) & (me >> 3)
    rank = (apart & 1) * 8 + ((apart >> 1) & 1) * 4 + ((along ^ 2) ^ swapped)
    return rank * per_owner + residue % per_owner


def outer_kernel(relative, n_inputs, n_handed, *refs):
    sources = refs[:n_inputs]
    keep_ref, send_ref = refs[n_inputs : n_inputs + 2]
    handed = refs[n_inputs + 2 : n_inputs + 2 + n_handed]
    own = n_inputs - n_handed
    targets = refs[n_inputs + 2 + n_handed :][:own]
    arrived, x_scratch, left_t_scratch, left_scratch, x_mat = refs[n_inputs + 2 + n_handed + own :]
    presence_ref, position_ref, gain_ref, bias_ref, first_ref, second_ref, coupling_ref = targets
    x_ref = handed[0]
    me = lax.axis_index("rows") if relative else None
    order = (handed[0],) + tuple(targets) + tuple(handed[1:])
    copies = [
        pltpu.make_async_copy(source, target, arrived.at[n])
        for n, (source, target) in enumerate(zip(sources, order))
    ]
    for copy in copies[: own + 1]:
        copy.start()
    rows, residues, channels = x_ref.shape
    hidden = first_ref.shape[0]
    half = residues // 2
    per_owner = residues // OWNERS
    quad = LANES // hidden
    groups = hidden // quad
    square = (residues, residues)

    averaging = mean_matrix(channels)
    lanes = iota((residues, half * 2 * channels), 1)
    wanted = lanes // (2 * channels) + half * ((lanes % (2 * channels)) // channels)
    spread = jnp.where(iota(lanes.shape, 0) == wanted, 1.0, 0.0).astype(BF16)
    diagonal = iota(square, 0) == iota(square, 1)
    order = (place(iota(square, 1), me, per_owner) == iota(square, 0)).astype(BF16)

    for copy in copies[own + 1 :]:
        copy.start()
    for copy in copies[: own + 1]:
        copy.wait()
    x_scratch[...] = two_halves(x_ref[...], half).astype(F32).reshape(rows * half, 2 * channels)
    tokens = jnp.concatenate(
        [x_scratch[pl.ds(p, rows, stride=half), :] for p in range(half)], axis=0
    ).astype(BF16)
    normed = standardize_pairs(tokens, averaging, twice(gain_ref[...]), twice(bias_ref[...]))

    position = jnp.where(diagonal, position_ref[...].astype(F32), 0.0).sum(axis=1, keepdims=True)
    valid = (presence_ref[...].astype(F32) * position).astype(BF16)
    flags = dot(valid, spread, ((0,), (0,)))
    flags = jnp.concatenate(
        [flags[:, p * 2 * channels : (p + 1) * 2 * channels] for p in range(half)], axis=0
    )
    normed = (normed * flags).astype(BF16)

    left_t = dot(block_pair(first_ref[...]), normed, ((1,), (1,)))
    for v in range(left_t_scratch.shape[0]):
        left_t_scratch[v] = left_t[:, v * LANES : (v + 1) * LANES]
    low = iota((groups, LANES), 1) < rows
    per = LANES // rows
    for side in range(2):
        for v in range(half // per):
            pieces = [
                left_t_scratch[v, pl.ds(side * hidden + h4, groups, stride=quad), :]
                for h4 in range(quad)
            ]
            turned = [pltpu.roll(piece, rows, 1) for piece in pieces]
            for odd in range(2):
                row = place(side * half + v * per + odd, me, per_owner)
                for c in range(quad // 2):
                    if odd:
                        tile = jnp.where(low, turned[2 * c], pieces[2 * c + 1])
                    else:
                        tile = jnp.where(low, pieces[2 * c], turned[2 * c + 1])
                    left_scratch[c, pl.ds(row, groups, stride=residues), :] = tile
    left = jnp.concatenate(
        [left_scratch[c] for c in range(quad // 2)], axis=1
    ).astype(BF16)

    repeated = jnp.concatenate([second_ref[...]] * quad, axis=0)
    right = dot(normed, block_pair(repeated), ((1,), (1,))).astype(BF16)
    lane_group = iota((rows, LANES), 1) // hidden
    masks = [lane_group == h4 for h4 in range(quad)]
    zero = jnp.zeros((rows, LANES), BF16)
    for j in range(0, residues, JOIN):
        beside = []
        for one_j in range(j, j + JOIN):
            side, p = one_j // half, one_j % half
            one = right[p * rows : (p + 1) * rows, side * LANES : (side + 1) * LANES]
            beside.append(jnp.concatenate([jnp.where(m, one, zero) for m in masks], axis=0))
        product = dot(left, jnp.concatenate(beside, axis=1)).astype(BF16)
        for n in range(JOIN):
            for g in range(groups):
                x_mat[(j + n) * residues : (j + n + 1) * residues, g * LANES : (g + 1) * LANES] = product[
                    g * residues : (g + 1) * residues, n * LANES : (n + 1) * LANES
                ]
    coupling = coupling_ref[...]
    projected = jnp.concatenate(
        [
            dot(x_mat[at : at + CHUNK, :], coupling) for at in range(0, residues * residues, CHUNK)
        ], axis=0,
    )
    counts = dot(dot(order, valid).astype(BF16), valid, ((1,), (1,)))
    counts = jnp.concatenate([counts, jnp.zeros((residues, LANES - residues), F32)], axis=1)
    for j in range(residues):
        rows_j = counts if j == residues - 1 else projected[j * residues : (j + 1) * residues, :]
        keep_ref[pl.ds(j, half, stride=residues), :] = rows_j[:half]
        send_ref[pl.ds(j, half, stride=residues), :] = rows_j[half:]
    for copy in copies[own + 1 :]:
        copy.wait()


def transition_rows(x_ref, start, count, gain_ref, bias_ref, switch_ref, expand_ref, contract_ref, out_ref):
    _, residues, channels = x_ref.shape
    half = residues // 2
    averaging = mean_matrix(channels)
    gain, bias = twice(gain_ref[...]), twice(bias_ref[...])
    switch = block_pair(switch_ref[...])
    expand = block_pair(expand_ref[...])
    contract = block_pair(contract_ref[...])
    for at in range(0, count, STEP):
        pairs = two_halves(x_ref[start + at : start + at + STEP], half).reshape(STEP * half, 2 * channels)
        normed = standardize_pairs(pairs, averaging, gain, bias).astype(BF16)
        gate = dot(normed, switch) * 0.5
        inner = ((gate + gate * jnp.tanh(gate)) * dot(normed, expand)).astype(BF16)
        result = (pairs.astype(F32) + dot(inner, contract, ((1,), (1,)))).astype(BF16)
        result = result.reshape(STEP, half, 2 * channels)
        out_ref[at : at + STEP, :half, :] = result[:, :, :channels]
        out_ref[at : at + STEP, half:, :] = result[:, :, channels:]
        yield at


def transition_part(start, x_ref, *refs):
    *weight_refs, out_ref = refs
    for _ in transition_rows(x_ref, start, out_ref.shape[0], *weight_refs, out_ref):
        pass


def transition_last(n_parts, x_ref, *refs):
    weight_refs = refs[: -3 - n_parts]
    part_refs = refs[-3 - n_parts : -3]
    out_hbm, result_ref, sent = refs[-3:]
    copies = []

    def send(source, at, count):
        copies.append(pltpu.make_async_copy(source, out_hbm.at[pl.ds(at, count)], sent.at[len(copies)]))
        copies[-1].start()

    head = 0
    for part_ref in part_refs:
        send(part_ref, head, part_ref.shape[0])
        head += part_ref.shape[0]
    for at in transition_rows(x_ref, head, result_ref.shape[0], *weight_refs, result_ref):
        send(result_ref.at[pl.ds(at, STEP)], head + at, STEP)
    for copy in copies:
        copy.wait()


def finish_kernel(residues, *refs):
    *summand_refs, offset_ref, out_ref = refs
    total = summand_refs[0][...]
    for ref in summand_refs[1:]:
        total = total + ref[...]
    square = (residues, residues)
    diagonal = iota(square, 0) == iota(square, 1)
    last = iota((residues, total.shape[1]), 0) == residues - 1
    for start in range(0, total.shape[0], residues):
        block = total[start : start + residues]
        counts = jnp.where(diagonal, block[residues - 1 :, :residues], 0.0).sum(axis=1, keepdims=True)
        mean = jnp.where(last, 0.0, block) / jnp.maximum(counts, 1.0)
        out_ref[start : start + residues, :] = mean + offset_ref[...]


def pick(array, index, axis):
    return lax.dynamic_index_in_dim(array, index, axis, keepdims=False)


def swap(array, size, apart):
    return lax.ppermute(array, "rows", [(i, i ^ apart) for i in range(size)])


def hop(array, size, targets):
    step = size // len(targets)
    return lax.ppermute(array, "rows", [(i, targets[i // step] * step + i % step) for i in range(size)])


def scatter_sum(partial, size):
    me = lax.axis_index("rows")
    tail = partial.shape[1:]
    done = 1
    while size // done > 4 or (size // done) % 4:
        parts = partial.reshape((size // done // 2, 2) + tail)
        mine = (me // done) % 2
        partial = pick(parts, mine, 1) + swap(pick(parts, 1 - mine, 1), size, done)
        done *= 2
    mine = me // done
    total = pick(partial, mine, 0)
    for k in range(1, size // done):
        total = total + swap(pick(partial, mine ^ k, 0), size, k * done)
    return total


def inside(shape, dtype):
    return pltpu.VMEM(shape, dtype)


def transition(features, weights, start, count, parts=()):
    rows, residues, channels = features.shape
    operands = [features, *weights, *parts]
    last = start + count == rows
    return pl.pallas_call(
        functools.partial(transition_last, len(parts)) if last else functools.partial(transition_part, start),
        out_shape=jax.ShapeDtypeStruct(features.shape, BF16) if last else inside((count, residues, channels), BF16),
        in_specs=[pl.BlockSpec(memory_space=pltpu.VMEM)] * len(operands),
        out_specs=pl.BlockSpec(memory_space=pltpu.HBM if last else pltpu.VMEM),
        scratch_shapes=[
            pltpu.VMEM((count, residues, channels), BF16),
            pltpu.SemaphoreType.DMA((len(parts) + count // STEP,)),
        ] if last else [],
        compiler_params=pltpu.CompilerParams(vmem_limit_bytes=VMEM_LIMIT),
        cost_estimate=pl.CostEstimate(
            flops=6_000_000 * count, bytes_accessed=30_000 * count, transcendentals=8_000 * count
        ),
        name="transition_last" if last else "transition_part",
    )(*(pltpu.with_memory_space_constraint(a, pltpu.VMEM) for a in operands))


def body(
    sequence_features,
    sequence_presence,
    position_presence,
    product_scale_vector,
    product_shift_vector,
    first_factor_matrix,
    second_factor_matrix,
    coupling_matrix,
    coupling_offset,
    feedforward_scale_vector,
    feedforward_shift_vector,
    feedforward_switch_matrix,
    feedforward_expand_matrix,
    feedforward_contract_matrix,
    *,
    size,
):
    rows, residues, channels = sequence_features.shape
    hidden = first_factor_matrix.shape[1]
    pair_channels = coupling_matrix.shape[1]
    pairs = residues * residues
    own = pairs // size
    relative = size == OWNERS
    row = lambda v: v.reshape(1, -1)
    used = (
        sequence_presence.T,
        row(position_presence),
        row(product_scale_vector),
        row(product_shift_vector),
        first_factor_matrix.T,
        second_factor_matrix.T,
        coupling_matrix,
    )
    handed = (
        sequence_features,
        row(coupling_offset),
        row(feedforward_scale_vector),
        row(feedforward_shift_vector),
        feedforward_switch_matrix,
        feedforward_expand_matrix,
        feedforward_contract_matrix.T,
    )
    operands = handed[:1] + used + handed[1:]
    results = [inside((pairs // 2, pair_channels), F32)] * 2
    results += [inside(operand.shape, operand.dtype) for operand in handed]
    keep, send, features, offset, *weights = pl.pallas_call(
        functools.partial(outer_kernel, relative, len(operands), len(handed)),
        out_shape=results,
        in_specs=[pl.BlockSpec(memory_space=pltpu.HBM)] * len(operands),
        out_specs=[pl.BlockSpec(memory_space=pltpu.VMEM)] * len(results),
        scratch_shapes=[pltpu.VMEM(operand.shape, operand.dtype) for operand in used] + [
            pltpu.SemaphoreType.DMA((len(operands),)),
            pltpu.VMEM((rows * residues // 2, 2 * channels), F32),
            pltpu.VMEM((rows * residues // 2 // LANES, 2 * hidden, LANES), F32),
            pltpu.VMEM((rows // hidden, pairs * hidden // LANES, LANES), F32),
            pltpu.VMEM((pairs, hidden * hidden), BF16),
        ],
        compiler_params=pltpu.CompilerParams(vmem_limit_bytes=VMEM_LIMIT),
        name="outer_products",
    )(*(pltpu.with_memory_space_constraint(operand, pltpu.HBM) for operand in operands))
    if relative:
        keep = keep.reshape(2, 4, own, pair_channels)
        first = transition(features, weights, 0, rows // 4)
        got, first = lax.optimization_barrier((swap(send, size, 1), first))
        got = got.reshape(2, 4, own, pair_channels)
        away = keep[1] + got[1]
        far_away, features = lax.optimization_barrier((away[:2], features))
        far = swap(far_away, size, 2)
        second = transition(features, weights, rows // 4, rows // 4)
        near_away, second = lax.optimization_barrier((away[2:], second))
        near = swap(near_away, size, 2)
        here = keep[0] + got[0]
        upper = here[:2] + far
        two, three = hop(upper[0], size, FIRST_HOP), hop(upper[1], size, SECOND_HOP)
        lower = here[2:] + near
        one = swap(lower[1], size, 4)
        refreshed = transition(features, weights, rows // 2, rows // 2, (first, second))
        summands = (two, three, one, lower[0])
        pair_mean_update = pl.pallas_call(
            functools.partial(finish_kernel, residues),
            out_shape=jax.ShapeDtypeStruct((own, pair_channels), F32),
            in_specs=[pl.BlockSpec(memory_space=pltpu.VMEM)] * (len(summands) + 1),
            compiler_params=pltpu.CompilerParams(vmem_limit_bytes=VMEM_LIMIT),
            name="finish",
        )(*(pltpu.with_memory_space_constraint(a, pltpu.VMEM) for a in summands + (offset,)))
    else:
        refreshed = transition(features, weights, 0, rows)
        grid = jnp.concatenate([keep.reshape(residues // 2, residues, pair_channels),
                                send.reshape(residues // 2, residues, pair_channels)], axis=0)
        counted = lax.psum(grid[:, residues - 1, :residues], "rows").reshape(size, own)
        counted = pick(counted, lax.axis_index("rows"), 0)[:, None]
        last = iota(grid.shape, 1) == residues - 1
        summed = scatter_sum(jnp.where(last, 0.0, grid).reshape(size, own, pair_channels), size)
        pair_mean_update = summed / jnp.maximum(counted, 1.0) + coupling_offset
    return pair_mean_update, refreshed


def solution(mesh):
    in_specs = (
        P(("groups", "rows"), None, None),
        P(("groups", "rows"), None),
        P("groups"),
    ) + (P(),) * 11
    out_specs = (P(("groups", "rows"), None), P(("groups", "rows"), None, None))
    return jax.shard_map(
        functools.partial(body, size=mesh.shape["rows"]),
        mesh=mesh, in_specs=in_specs, out_specs=out_specs, check_vma=False,
    )
```

```python
import functools

import jax
import jax.numpy as jnp
from jax import lax
from jax.experimental import pallas as pl
from jax.experimental.pallas import tpu as pltpu
from jax.sharding import PartitionSpec as P

F32 = jnp.float32
BF16 = jnp.bfloat16
EPS = 1e-05
LANES = 128
VMEM_LIMIT = 48 * 1024 * 1024
STEP = 16
JOIN = 2
CHUNK = 512
FIRST_HOP = (2, 3, 1, 0)
SECOND_HOP = (3, 2, 0, 1)
LAST_HOP = (1, 0, 3, 2)
TURNED = 0b0001
UNLIKE = 1
OWNERS = 16


def dot(a, b, dims=((1,), (0,))):
    return lax.dot_general(a, b, (dims, ((), ())), preferred_element_type=F32)


def two_halves(array, half):
    return jnp.concatenate([array[:, :half, :], array[:, half:, :]], axis=-1)


def twice(vector):
    return jnp.concatenate([vector, vector], axis=-1)


def block_pair(matrix):
    zero = jnp.zeros_like(matrix)
    return jnp.concatenate(
        [jnp.concatenate([matrix, zero], axis=1), jnp.concatenate([zero, matrix], axis=1)], axis=0
    )


def iota(shape, axis):
    return lax.broadcasted_iota(jnp.int32, shape, axis)


def mean_matrix(channels):
    shape = (2 * channels, 2 * channels)
    same = iota(shape, 0) // channels == iota(shape, 1) // channels
    return jnp.where(same, 1.0 / channels, 0.0).astype(BF16)


def standardize_pairs(values, averaging, gain, bias):
    centered = values.astype(F32) - dot(values, averaging)
    variance = dot((centered * centered).astype(BF16), averaging)
    return centered * lax.rsqrt(variance + EPS) * gain + bias


def ranks_along_z():
    table = 0
    for z, order in enumerate(zip(FIRST_HOP, SECOND_HOP, range(len(FIRST_HOP)), LAST_HOP)):
        for place_of, other in enumerate(order):
            table |= place_of << (z * 8 + (z ^ other) * 2)
    return table - (1 << 32) if table >> 31 else table


RANKS = ranks_along_z()


def relabel(device):
    return device ^ ((TURNED >> (device >> 2)) & 1)


def place(residue, me, per_owner):
    if me is None:
        return residue
    apart = relabel(residue // per_owner) ^ relabel(me)
    along_y = (apart >> 1) & 1
    along_z = (RANKS >> ((me >> 2) * 8 + (apart >> 2) * 2)) & 3
    rank = (((apart & 1) ^ (along_y & UNLIKE)) * 2 + along_y) * 4 + along_z
    return rank * per_owner + residue % per_owner


def outer_half(left, right, coupling, counts, x_mat, *out_refs):
    count = counts.shape[0]
    part = count // len(out_refs)
    residues = out_refs[0].shape[0] // part
    half = residues // 2
    groups = left.shape[0] // count
    rows = right.shape[0] // half
    quad = left.shape[1] // rows
    lane_group = iota((rows, LANES), 1) // (LANES // quad)
    masks = [lane_group == h4 for h4 in range(quad)]
    zero = jnp.zeros((rows, LANES), BF16)
    for j in range(0, residues, JOIN):
        beside = []
        for one_j in range(j, j + JOIN):
            side, p = one_j // half, one_j % half
            one = right[p * rows : (p + 1) * rows, side * LANES : (side + 1) * LANES]
            beside.append(jnp.concatenate([jnp.where(m, one, zero) for m in masks], axis=0))
        product = dot(left, jnp.concatenate(beside, axis=1)).astype(BF16)
        for n in range(JOIN):
            for g in range(groups):
                x_mat[(j + n) * count : (j + n + 1) * count, g * LANES : (g + 1) * LANES] = product[
                    g * count : (g + 1) * count, n * LANES : (n + 1) * LANES
                ]
    projected = [
        dot(x_mat[at : at + CHUNK, :], coupling) for at in range(0, residues * count, CHUNK)
    ]
    projected = jnp.concatenate(projected, axis=0)
    for j in range(residues):
        rows_j = counts if j == residues - 1 else projected[j * count : (j + 1) * count, :]
        for n, out_ref in enumerate(out_refs):
            out_ref[pl.ds(j, part, stride=residues), :] = rows_j[n * part : (n + 1) * part]


def outer_second_kernel(left_ref, right_ref, coupling_ref, counts_ref, here_ref, away_ref, x_mat):
    outer_half(left_ref[...], right_ref[...], coupling_ref[...], counts_ref[...], x_mat, here_ref, away_ref)


def outer_kernel(relative, n_inputs, n_handed, *refs):
    sources = refs[:n_inputs]
    outs, refs = refs[n_inputs : n_inputs + 5], refs[n_inputs + 5 :]
    here_ref, away_ref, left_ref, right_ref, counts_ref = outs
    handed = refs[:n_handed]
    own = n_inputs - n_handed
    early = own + 2
    targets = refs[n_handed : n_handed + own]
    arrived, x_scratch, left_t_scratch, left_scratch, x_mat = refs[n_handed + own :]
    presence_ref, position_ref, gain_ref, bias_ref, first_ref, second_ref = targets
    x_ref, coupling_ref = handed[:2]
    me = lax.axis_index("rows") if relative else None
    order = (handed[0],) + tuple(targets) + tuple(handed[1:])
    copies = [
        pltpu.make_async_copy(source, target, arrived.at[n])
        for n, (source, target) in enumerate(zip(sources, order))
    ]
    for copy in copies[:early]:
        copy.start()
    rows, residues, channels = x_ref.shape
    hidden = first_ref.shape[0]
    half = residues // 2
    per_owner = residues // OWNERS
    quad = LANES // hidden
    groups = hidden // quad
    square = (residues, residues)

    averaging = mean_matrix(channels)
    lanes = iota((residues, half * 2 * channels), 1)
    wanted = lanes // (2 * channels) + half * ((lanes % (2 * channels)) // channels)
    spread = jnp.where(iota(lanes.shape, 0) == wanted, 1.0, 0.0).astype(BF16)
    diagonal = iota(square, 0) == iota(square, 1)
    order = (place(iota(square, 1), me, per_owner) == iota(square, 0)).astype(BF16)

    for copy in copies[early:]:
        copy.start()
    for copy in copies[:early]:
        copy.wait()
    x_scratch[...] = two_halves(x_ref[...], half).astype(F32).reshape(rows * half, 2 * channels)
    tokens = jnp.concatenate(
        [x_scratch[pl.ds(p, rows, stride=half), :] for p in range(half)], axis=0
    ).astype(BF16)
    normed = standardize_pairs(tokens, averaging, twice(gain_ref[...]), twice(bias_ref[...]))

    position = jnp.where(diagonal, position_ref[...].astype(F32), 0.0).sum(axis=1, keepdims=True)
    valid = (presence_ref[...].astype(F32) * position).astype(BF16)
    flags = dot(valid, spread, ((0,), (0,)))
    flags = jnp.concatenate(
        [flags[:, p * 2 * channels : (p + 1) * 2 * channels] for p in range(half)], axis=0
    )
    normed = (normed * flags).astype(BF16)

    left_t = dot(block_pair(first_ref[...]), normed, ((1,), (1,)))
    for v in range(left_t_scratch.shape[0]):
        left_t_scratch[v] = left_t[:, v * LANES : (v + 1) * LANES]
    low = iota((groups, LANES), 1) < rows
    per = LANES // rows
    for side in range(2):
        for v in range(half // per):
            pieces = [
                left_t_scratch[v, pl.ds(side * hidden + h4, groups, stride=quad), :]
                for h4 in range(quad)
            ]
            turned = [pltpu.roll(piece, rows, 1) for piece in pieces]
            for odd in range(2):
                row = place(side * half + v * per + odd, me, per_owner)
                for c in range(quad // 2):
                    if odd:
                        tile = jnp.where(low, turned[2 * c], pieces[2 * c + 1])
                    else:
                        tile = jnp.where(low, pieces[2 * c], turned[2 * c + 1])
                    at = (row // half) * (groups * half) + row % half
                    left_scratch[c, pl.ds(at, groups, stride=half), :] = tile
    left = jnp.concatenate(
        [left_scratch[c] for c in range(quad // 2)], axis=1
    ).astype(BF16)

    repeated = jnp.concatenate([second_ref[...]] * quad, axis=0)
    right = dot(normed, block_pair(repeated), ((1,), (1,))).astype(BF16)
    right_ref[...] = right
    left_ref[...] = left[: groups * half]
    counts = dot(dot(order, valid).astype(BF16), valid, ((1,), (1,)))
    counts = jnp.concatenate([counts, jnp.zeros((residues, LANES - residues), F32)], axis=1)
    counts_ref[...] = counts[:half]
    outer_half(left[groups * half :], right, coupling_ref[...], counts[half:], x_mat, here_ref, away_ref)
    for copy in copies[early:]:
        copy.wait()


def transition_rows(x_ref, start, count, gain_ref, bias_ref, switch_ref, expand_ref, contract_ref, out_ref):
    _, residues, channels = x_ref.shape
    half = residues // 2
    averaging = mean_matrix(channels)
    gain, bias = twice(gain_ref[...]), twice(bias_ref[...])
    switch = block_pair(switch_ref[...])
    expand = block_pair(expand_ref[...])
    contract = block_pair(contract_ref[...])
    for at in range(0, count, STEP):
        pairs = two_halves(x_ref[start + at : start + at + STEP], half).reshape(STEP * half, 2 * channels)
        normed = standardize_pairs(pairs, averaging, gain, bias).astype(BF16)
        gate = dot(normed, switch) * 0.5
        inner = ((gate + gate * jnp.tanh(gate)) * dot(normed, expand)).astype(BF16)
        result = (pairs.astype(F32) + dot(inner, contract, ((1,), (1,)))).astype(BF16)
        result = result.reshape(STEP, half, 2 * channels)
        out_ref[at : at + STEP, :half, :] = result[:, :, :channels]
        out_ref[at : at + STEP, half:, :] = result[:, :, channels:]
        yield at


def transition_part(start, x_ref, *refs):
    *weight_refs, out_ref = refs
    for _ in transition_rows(x_ref, start, out_ref.shape[0], *weight_refs, out_ref):
        pass


def transition_last(n_parts, x_ref, *refs):
    weight_refs = refs[: -3 - n_parts]
    part_refs = refs[-3 - n_parts : -3]
    out_hbm, result_ref, sent = refs[-3:]
    copies = []

    def send(source, at, count):
        copies.append(pltpu.make_async_copy(source, out_hbm.at[pl.ds(at, count)], sent.at[len(copies)]))
        copies[-1].start()

    head = 0
    for part_ref in part_refs:
        send(part_ref, head, part_ref.shape[0])
        head += part_ref.shape[0]
    for at in transition_rows(x_ref, head, result_ref.shape[0], *weight_refs, result_ref):
        send(result_ref.at[pl.ds(at, STEP)], head + at, STEP)
    for copy in copies:
        copy.wait()


def finish_kernel(residues, *refs):
    *summand_refs, offset_ref, out_ref = refs
    total = summand_refs[0][...]
    for ref in summand_refs[1:]:
        total = total + ref[...]
    square = (residues, residues)
    diagonal = iota(square, 0) == iota(square, 1)
    last = iota((residues, total.shape[1]), 0) == residues - 1
    for start in range(0, total.shape[0], residues):
        block = total[start : start + residues]
        counts = jnp.where(diagonal, block[residues - 1 :, :residues], 0.0).sum(axis=1, keepdims=True)
        mean = jnp.where(last, 0.0, block) / jnp.maximum(counts, 1.0)
        out_ref[start : start + residues, :] = mean + offset_ref[...]


def pick(array, index, axis):
    return lax.dynamic_index_in_dim(array, index, axis, keepdims=False)


def swap(array, size, apart):
    return lax.ppermute(array, "rows", [(i, i ^ apart) for i in range(size)])


def hop(array, size, targets):
    step = size // len(targets)
    pairs = [(i, relabel(targets[i // step] * step + relabel(i) % step)) for i in range(size)]
    return lax.ppermute(array, "rows", pairs)


def scatter_sum(partial, size):
    me = lax.axis_index("rows")
    tail = partial.shape[1:]
    done = 1
    while size // done > 4 or (size // done) % 4:
        parts = partial.reshape((size // done // 2, 2) + tail)
        mine = (me // done) % 2
        partial = pick(parts, mine, 1) + swap(pick(parts, 1 - mine, 1), size, done)
        done *= 2
    mine = me // done
    total = pick(partial, mine, 0)
    for k in range(1, size // done):
        total = total + swap(pick(partial, mine ^ k, 0), size, k * done)
    return total


def inside(shape, dtype):
    return pltpu.VMEM(shape, dtype)


def transition(features, weights, start, count, parts=()):
    rows, residues, channels = features.shape
    operands = [features, *weights, *parts]
    last = start + count == rows
    return pl.pallas_call(
        functools.partial(transition_last, len(parts)) if last else functools.partial(transition_part, start),
        out_shape=jax.ShapeDtypeStruct(features.shape, BF16) if last else inside((count, residues, channels), BF16),
        in_specs=[pl.BlockSpec(memory_space=pltpu.VMEM)] * len(operands),
        out_specs=pl.BlockSpec(memory_space=pltpu.HBM if last else pltpu.VMEM),
        scratch_shapes=[
            pltpu.VMEM((count, residues, channels), BF16),
            pltpu.SemaphoreType.DMA((len(parts) + count // STEP,)),
        ] if last else [],
        compiler_params=pltpu.CompilerParams(vmem_limit_bytes=VMEM_LIMIT),
        cost_estimate=pl.CostEstimate(
            flops=6_000_000 * count, bytes_accessed=30_000 * count, transcendentals=8_000 * count
        ),
        name="transition_last" if last else "transition_part",
    )(*(pltpu.with_memory_space_constraint(a, pltpu.VMEM) for a in operands))


def body(
    sequence_features,
    sequence_presence,
    position_presence,
    product_scale_vector,
    product_shift_vector,
    first_factor_matrix,
    second_factor_matrix,
    coupling_matrix,
    coupling_offset,
    feedforward_scale_vector,
    feedforward_shift_vector,
    feedforward_switch_matrix,
    feedforward_expand_matrix,
    feedforward_contract_matrix,
    *,
    size,
):
    rows, residues, channels = sequence_features.shape
    hidden = first_factor_matrix.shape[1]
    pair_channels = coupling_matrix.shape[1]
    pairs = residues * residues
    own = pairs // size
    relative = size == OWNERS
    row = lambda v: v.reshape(1, -1)
    used = (
        sequence_presence.T,
        row(position_presence),
        row(product_scale_vector),
        row(product_shift_vector),
        first_factor_matrix.T,
        second_factor_matrix.T,
    )
    handed = (
        sequence_features,
        coupling_matrix,
        row(coupling_offset),
        row(feedforward_scale_vector),
        row(feedforward_shift_vector),
        feedforward_switch_matrix,
        feedforward_expand_matrix,
        feedforward_contract_matrix.T,
    )
    operands = handed[:1] + used + handed[1:]
    split = (pairs * hidden // LANES // 2, rows * LANES // hidden)
    results = [
        inside((pairs // 4, pair_channels), F32),
        inside((pairs // 4, pair_channels), F32),
        inside(split, BF16),
        inside((rows * residues // 2, 2 * LANES), BF16),
        inside((residues // 2, LANES), F32),
    ]
    results += [inside(operand.shape, operand.dtype) for operand in handed]
    send_here, send_away, left, right, counts, features, coupling, offset, *weights = pl.pallas_call(
        functools.partial(outer_kernel, relative, len(operands), len(handed)),
        out_shape=results,
        in_specs=[pl.BlockSpec(memory_space=pltpu.HBM)] * len(operands),
        out_specs=[pl.BlockSpec(memory_space=pltpu.VMEM)] * len(results),
        scratch_shapes=[pltpu.VMEM(operand.shape, operand.dtype) for operand in used] + [
            pltpu.SemaphoreType.DMA((len(operands),)),
            pltpu.VMEM((rows * residues // 2, 2 * channels), F32),
            pltpu.VMEM((rows * residues // 2 // LANES, 2 * hidden, LANES), F32),
            pltpu.VMEM((rows // hidden, pairs * hidden // LANES, LANES), F32),
            pltpu.VMEM((pairs // 2, hidden * hidden), BF16),
        ],
        compiler_params=pltpu.CompilerParams(vmem_limit_bytes=VMEM_LIMIT),
        name="outer_products",
    )(*(pltpu.with_memory_space_constraint(operand, pltpu.HBM) for operand in operands))
    kept = (left, right, coupling, counts)
    keep_here, keep_away = pl.pallas_call(
        outer_second_kernel,
        out_shape=[inside((pairs // 4, pair_channels), F32)] * 2,
        in_specs=[pl.BlockSpec(memory_space=pltpu.VMEM)] * len(kept),
        out_specs=[pl.BlockSpec(memory_space=pltpu.VMEM)] * 2,
        scratch_shapes=[pltpu.VMEM((pairs // 2, hidden * hidden), BF16)],
        compiler_params=pltpu.CompilerParams(vmem_limit_bytes=VMEM_LIMIT),
        cost_estimate=pl.CostEstimate(flops=1_000_000_000, bytes_accessed=2_000_000, transcendentals=0),
        name="outer_second",
    )(*(pltpu.with_memory_space_constraint(a, pltpu.VMEM) for a in kept))
    if relative:
        got_here = swap(send_here, size, 1)
        got_away, keep_away = lax.optimization_barrier((swap(send_away, size, 1), keep_away))
        away = (keep_away + got_away).reshape(4, own, pair_channels)
        far_away, features = lax.optimization_barrier((away[:2], features))
        far = swap(far_away, size, 2 + UNLIKE)
        first = transition(features, weights, 0, rows // 4)
        near_away, first = lax.optimization_barrier((away[2:], first))
        near = swap(near_away, size, 2 + UNLIKE)
        here = (keep_here + got_here).reshape(4, own, pair_channels)
        upper = here[:2] + far
        two, three = hop(upper[0], size, FIRST_HOP), hop(upper[1], size, SECOND_HOP)
        lower = here[2:] + near
        one = hop(lower[1], size, LAST_HOP)
        refreshed = transition(features, weights, rows // 4, rows - rows // 4, (first,))
        summands = (three, two, one, lower[0])
        pair_mean_update = pl.pallas_call(
            functools.partial(finish_kernel, residues),
            out_shape=jax.ShapeDtypeStruct((own, pair_channels), F32),
            in_specs=[pl.BlockSpec(memory_space=pltpu.VMEM)] * (len(summands) + 1),
            compiler_params=pltpu.CompilerParams(vmem_limit_bytes=VMEM_LIMIT),
            name="finish",
        )(*(pltpu.with_memory_space_constraint(a, pltpu.VMEM) for a in summands + (offset,)))
    else:
        refreshed = transition(features, weights, 0, rows)
        grid = jnp.concatenate([keep_here, keep_away, send_here, send_away], axis=0)
        grid = grid.reshape(residues, residues, pair_channels)
        counted = lax.psum(grid[:, residues - 1, :residues], "rows").reshape(size, own)
        counted = pick(counted, lax.axis_index("rows"), 0)[:, None]
        last = iota(grid.shape, 1) == residues - 1
        summed = scatter_sum(jnp.where(last, 0.0, grid).reshape(size, own, pair_channels), size)
        pair_mean_update = summed / jnp.maximum(counted, 1.0) + coupling_offset
    return pair_mean_update, refreshed


def solution(mesh):
    in_specs = (
        P(("groups", "rows"), None, None),
        P(("groups", "rows"), None),
        P("groups"),
    ) + (P(),) * 11
    out_specs = (P(("groups", "rows"), None), P(("groups", "rows"), None, None))
    return jax.shard_map(
        functools.partial(body, size=mesh.shape["rows"]),
        mesh=mesh, in_specs=in_specs, out_specs=out_specs, check_vma=False,
    )
```

```python
import functools

import jax
import jax.numpy as jnp
from jax import lax
from jax.experimental import pallas as pl
from jax.experimental.pallas import tpu as pltpu
from jax.sharding import PartitionSpec as P

F32 = jnp.float32
BF16 = jnp.bfloat16
EPS = 1e-05
LANES = 128
VMEM_LIMIT = 48 * 1024 * 1024
STEP = 16
JOIN = 2
CHUNK = 256
FIRST_HOP = (2, 3, 1, 0)
SECOND_HOP = (3, 2, 0, 1)
LAST_HOP = (1, 0, 3, 2)
TURNED = 0b0001
UNLIKE = 1
OWNERS = 16


def dot(a, b, dims=((1,), (0,))):
    return lax.dot_general(a, b, (dims, ((), ())), preferred_element_type=F32)


def two_halves(array, half):
    return jnp.concatenate([array[:, :half, :], array[:, half:, :]], axis=-1)


def twice(vector):
    return jnp.concatenate([vector, vector], axis=-1)


def block_pair(matrix):
    zero = jnp.zeros_like(matrix)
    return jnp.concatenate(
        [jnp.concatenate([matrix, zero], axis=1), jnp.concatenate([zero, matrix], axis=1)], axis=0
    )


def iota(shape, axis):
    return lax.broadcasted_iota(jnp.int32, shape, axis)


def mean_matrix(channels):
    shape = (2 * channels, 2 * channels)
    same = iota(shape, 0) // channels == iota(shape, 1) // channels
    return jnp.where(same, 1.0 / channels, 0.0).astype(BF16)


def standardize_pairs(values, averaging, gain, bias):
    centered = values.astype(F32) - dot(values, averaging)
    variance = dot((centered * centered).astype(BF16), averaging)
    return centered * lax.rsqrt(variance + EPS) * gain + bias


def ranks_along_z():
    table = 0
    for z, order in enumerate(zip(FIRST_HOP, SECOND_HOP, range(len(FIRST_HOP)), LAST_HOP)):
        for place_of, other in enumerate(order):
            table |= place_of << (z * 8 + (z ^ other) * 2)
    return table - (1 << 32) if table >> 31 else table


RANKS = ranks_along_z()


def relabel(device):
    return device ^ ((TURNED >> (device >> 2)) & 1)


def place(residue, me, per_owner):
    if me is None:
        return residue
    apart = relabel(residue // per_owner) ^ relabel(me)
    along_y = (apart >> 1) & 1
    along_z = (RANKS >> ((me >> 2) * 8 + (apart >> 2) * 2)) & 3
    rank = (((apart & 1) ^ (along_y & UNLIKE)) * 2 + along_y) * 4 + along_z
    return rank * per_owner + residue % per_owner


def outer_half(left, right, coupling, counts, x_mat, *out_refs):
    count = counts.shape[0]
    part = count // len(out_refs)
    residues = out_refs[0].shape[0] // part
    half = residues // 2
    groups = left.shape[0] // count
    rows = right.shape[0] // half
    quad = left.shape[1] // rows
    lane_group = iota((rows, LANES), 1) // (LANES // quad)
    masks = [lane_group == h4 for h4 in range(quad)]
    zero = jnp.zeros((rows, LANES), BF16)
    for j in range(0, residues, JOIN):
        beside = []
        for one_j in range(j, j + JOIN):
            side, p = one_j // half, one_j % half
            one = right[p * rows : (p + 1) * rows, side * LANES : (side + 1) * LANES]
            beside.append(jnp.concatenate([jnp.where(m, one, zero) for m in masks], axis=0))
        product = dot(left, jnp.concatenate(beside, axis=1)).astype(BF16)
        for n in range(JOIN):
            for g in range(groups):
                x_mat[(j + n) * count : (j + n + 1) * count, g * LANES : (g + 1) * LANES] = product[
                    g * count : (g + 1) * count, n * LANES : (n + 1) * LANES
                ]
    projected = [
        dot(x_mat[at : at + CHUNK, :], coupling) for at in range(0, residues * count, CHUNK)
    ]
    projected = jnp.concatenate(projected, axis=0)
    for j in range(residues):
        rows_j = counts if j == residues - 1 else projected[j * count : (j + 1) * count, :]
        for n, out_ref in enumerate(out_refs):
            out_ref[pl.ds(j, part, stride=residues), :] = rows_j[n * part : (n + 1) * part]


def outer_second_kernel(left_ref, right_ref, coupling_ref, counts_ref, here_ref, away_ref, x_mat):
    outer_half(left_ref[...], right_ref[...], coupling_ref[...], counts_ref[...], x_mat, here_ref, away_ref)


def outer_kernel(relative, n_inputs, n_handed, *refs):
    sources = refs[:n_inputs]
    outs, refs = refs[n_inputs : n_inputs + 5], refs[n_inputs + 5 :]
    here_ref, away_ref, left_ref, right_ref, counts_ref = outs
    handed = refs[:n_handed]
    own = n_inputs - n_handed
    early = own + 2
    targets = refs[n_handed : n_handed + own]
    arrived, x_scratch, left_t_scratch, left_scratch, x_mat = refs[n_handed + own :]
    presence_ref, position_ref, gain_ref, bias_ref, first_ref, second_ref = targets
    x_ref, coupling_ref = handed[:2]
    me = lax.axis_index("rows") if relative else None
    order = (handed[0],) + tuple(targets) + tuple(handed[1:])
    copies = [
        pltpu.make_async_copy(source, target, arrived.at[n])
        for n, (source, target) in enumerate(zip(sources, order))
    ]
    for copy in copies[:early]:
        copy.start()
    rows, residues, channels = x_ref.shape
    hidden = first_ref.shape[0]
    half = residues // 2
    per_owner = residues // OWNERS
    quad = LANES // hidden
    groups = hidden // quad
    square = (residues, residues)

    averaging = mean_matrix(channels)
    lanes = iota((residues, half * 2 * channels), 1)
    wanted = lanes // (2 * channels) + half * ((lanes % (2 * channels)) // channels)
    spread = jnp.where(iota(lanes.shape, 0) == wanted, 1.0, 0.0).astype(BF16)
    diagonal = iota(square, 0) == iota(square, 1)
    order = (place(iota(square, 1), me, per_owner) == iota(square, 0)).astype(BF16)

    for copy in copies[early:]:
        copy.start()
    for copy in copies[:early]:
        copy.wait()
    x_scratch[...] = two_halves(x_ref[...], half).astype(F32).reshape(rows * half, 2 * channels)
    tokens = jnp.concatenate(
        [x_scratch[pl.ds(p, rows, stride=half), :] for p in range(half)], axis=0
    ).astype(BF16)
    normed = standardize_pairs(tokens, averaging, twice(gain_ref[...]), twice(bias_ref[...]))

    position = jnp.where(diagonal, position_ref[...].astype(F32), 0.0).sum(axis=1, keepdims=True)
    valid = (presence_ref[...].astype(F32) * position).astype(BF16)
    flags = dot(valid, spread, ((0,), (0,)))
    flags = jnp.concatenate(
        [flags[:, p * 2 * channels : (p + 1) * 2 * channels] for p in range(half)], axis=0
    )
    normed = (normed * flags).astype(BF16)

    left_t = dot(block_pair(first_ref[...]), normed, ((1,), (1,)))
    for v in range(left_t_scratch.shape[0]):
        left_t_scratch[v] = left_t[:, v * LANES : (v + 1) * LANES]
    low = iota((groups, LANES), 1) < rows
    per = LANES // rows
    for side in range(2):
        for v in range(half // per):
            pieces = [
                left_t_scratch[v, pl.ds(side * hidden + h4, groups, stride=quad), :]
                for h4 in range(quad)
            ]
            turned = [pltpu.roll(piece, rows, 1) for piece in pieces]
            for odd in range(2):
                row = place(side * half + v * per + odd, me, per_owner)
                for c in range(quad // 2):
                    if odd:
                        tile = jnp.where(low, turned[2 * c], pieces[2 * c + 1])
                    else:
                        tile = jnp.where(low, pieces[2 * c], turned[2 * c + 1])
                    at = (row // half) * (groups * half) + row % half
                    left_scratch[c, pl.ds(at, groups, stride=half), :] = tile
    left = jnp.concatenate(
        [left_scratch[c] for c in range(quad // 2)], axis=1
    ).astype(BF16)

    repeated = jnp.concatenate([second_ref[...]] * quad, axis=0)
    right = dot(normed, block_pair(repeated), ((1,), (1,))).astype(BF16)
    right_ref[...] = right
    left_ref[...] = left[: groups * half]
    counts = dot(dot(order, valid).astype(BF16), valid, ((1,), (1,)))
    counts = jnp.concatenate([counts, jnp.zeros((residues, LANES - residues), F32)], axis=1)
    counts_ref[...] = counts[:half]
    outer_half(left[groups * half :], right, coupling_ref[...], counts[half:], x_mat, here_ref, away_ref)
    for copy in copies[early:]:
        copy.wait()


def transition_rows(x_ref, start, count, gain_ref, bias_ref, switch_ref, expand_ref, contract_ref, out_ref):
    _, residues, channels = x_ref.shape
    half = residues // 2
    averaging = mean_matrix(channels)
    gain, bias = twice(gain_ref[...]), twice(bias_ref[...])
    switch = block_pair(switch_ref[...])
    expand = block_pair(expand_ref[...])
    contract = block_pair(contract_ref[...])
    for at in range(0, count, STEP):
        pairs = two_halves(x_ref[start + at : start + at + STEP], half).reshape(STEP * half, 2 * channels)
        normed = standardize_pairs(pairs, averaging, gain, bias).astype(BF16)
        gate = dot(normed, switch) * 0.5
        inner = ((gate + gate * jnp.tanh(gate)) * dot(normed, expand)).astype(BF16)
        result = (pairs.astype(F32) + dot(inner, contract, ((1,), (1,)))).astype(BF16)
        result = result.reshape(STEP, half, 2 * channels)
        out_ref[at : at + STEP, :half, :] = result[:, :, :channels]
        out_ref[at : at + STEP, half:, :] = result[:, :, channels:]
        yield at


def transition_part(start, x_ref, *refs):
    *weight_refs, out_ref = refs
    for _ in transition_rows(x_ref, start, out_ref.shape[0], *weight_refs, out_ref):
        pass


def transition_last(n_parts, x_ref, *refs):
    weight_refs = refs[: -3 - n_parts]
    part_refs = refs[-3 - n_parts : -3]
    out_hbm, result_ref, sent = refs[-3:]
    copies = []

    def send(source, at, count):
        copies.append(pltpu.make_async_copy(source, out_hbm.at[pl.ds(at, count)], sent.at[len(copies)]))
        copies[-1].start()

    head = 0
    for part_ref in part_refs:
        send(part_ref, head, part_ref.shape[0])
        head += part_ref.shape[0]
    for at in transition_rows(x_ref, head, result_ref.shape[0], *weight_refs, result_ref):
        send(result_ref.at[pl.ds(at, STEP)], head + at, STEP)
    for copy in copies:
        copy.wait()


def finish_kernel(residues, *refs):
    *summand_refs, offset_ref, out_ref = refs
    total = summand_refs[0][...]
    for ref in summand_refs[1:]:
        total = total + ref[...]
    square = (residues, residues)
    diagonal = iota(square, 0) == iota(square, 1)
    last = iota((residues, total.shape[1]), 0) == residues - 1
    for start in range(0, total.shape[0], residues):
        block = total[start : start + residues]
        counts = jnp.where(diagonal, block[residues - 1 :, :residues], 0.0).sum(axis=1, keepdims=True)
        mean = jnp.where(last, 0.0, block) / jnp.maximum(counts, 1.0)
        out_ref[start : start + residues, :] = mean + offset_ref[...]


def pick(array, index, axis):
    return lax.dynamic_index_in_dim(array, index, axis, keepdims=False)


def swap(array, size, apart):
    return lax.ppermute(array, "rows", [(i, i ^ apart) for i in range(size)])


def hop(array, size, targets):
    step = size // len(targets)
    pairs = [(i, relabel(targets[i // step] * step + relabel(i) % step)) for i in range(size)]
    return lax.ppermute(array, "rows", pairs)


def scatter_sum(partial, size):
    me = lax.axis_index("rows")
    tail = partial.shape[1:]
    done = 1
    while size // done > 4 or (size // done) % 4:
        parts = partial.reshape((size // done // 2, 2) + tail)
        mine = (me // done) % 2
        partial = pick(parts, mine, 1) + swap(pick(parts, 1 - mine, 1), size, done)
        done *= 2
    mine = me // done
    total = pick(partial, mine, 0)
    for k in range(1, size // done):
        total = total + swap(pick(partial, mine ^ k, 0), size, k * done)
    return total


def inside(shape, dtype):
    return pltpu.VMEM(shape, dtype)


def transition(features, weights, start, count, parts=()):
    rows, residues, channels = features.shape
    operands = [features, *weights, *parts]
    last = start + count == rows
    return pl.pallas_call(
        functools.partial(transition_last, len(parts)) if last else functools.partial(transition_part, start),
        out_shape=jax.ShapeDtypeStruct(features.shape, BF16) if last else inside((count, residues, channels), BF16),
        in_specs=[pl.BlockSpec(memory_space=pltpu.VMEM)] * len(operands),
        out_specs=pl.BlockSpec(memory_space=pltpu.HBM if last else pltpu.VMEM),
        scratch_shapes=[
            pltpu.VMEM((count, residues, channels), BF16),
            pltpu.SemaphoreType.DMA((len(parts) + count // STEP,)),
        ] if last else [],
        compiler_params=pltpu.CompilerParams(vmem_limit_bytes=VMEM_LIMIT),
        cost_estimate=pl.CostEstimate(
            flops=6_000_000 * count, bytes_accessed=30_000 * count, transcendentals=8_000 * count
        ),
        name="transition_last" if last else "transition_part",
    )(*(pltpu.with_memory_space_constraint(a, pltpu.VMEM) for a in operands))


def body(
    sequence_features,
    sequence_presence,
    position_presence,
    product_scale_vector,
    product_shift_vector,
    first_factor_matrix,
    second_factor_matrix,
    coupling_matrix,
    coupling_offset,
    feedforward_scale_vector,
    feedforward_shift_vector,
    feedforward_switch_matrix,
    feedforward_expand_matrix,
    feedforward_contract_matrix,
    *,
    size,
):
    rows, residues, channels = sequence_features.shape
    hidden = first_factor_matrix.shape[1]
    pair_channels = coupling_matrix.shape[1]
    pairs = residues * residues
    own = pairs // size
    relative = size == OWNERS
    row = lambda v: v.reshape(1, -1)
    used = (
        sequence_presence.T,
        row(position_presence),
        row(product_scale_vector),
        row(product_shift_vector),
        first_factor_matrix.T,
        second_factor_matrix.T,
    )
    handed = (
        sequence_features,
        coupling_matrix,
        row(coupling_offset),
        row(feedforward_scale_vector),
        row(feedforward_shift_vector),
        feedforward_switch_matrix,
        feedforward_expand_matrix,
        feedforward_contract_matrix.T,
    )
    operands = handed[:1] + used + handed[1:]
    split = (pairs * hidden // LANES // 2, rows * LANES // hidden)
    results = [
        inside((pairs // 4, pair_channels), F32),
        inside((pairs // 4, pair_channels), F32),
        inside(split, BF16),
        inside((rows * residues // 2, 2 * LANES), BF16),
        inside((residues // 2, LANES), F32),
    ]
    results += [inside(operand.shape, operand.dtype) for operand in handed]
    send_here, send_away, left, right, counts, features, coupling, offset, *weights = pl.pallas_call(
        functools.partial(outer_kernel, relative, len(operands), len(handed)),
        out_shape=results,
        in_specs=[pl.BlockSpec(memory_space=pltpu.HBM)] * len(operands),
        out_specs=[pl.BlockSpec(memory_space=pltpu.VMEM)] * len(results),
        scratch_shapes=[pltpu.VMEM(operand.shape, operand.dtype) for operand in used] + [
            pltpu.SemaphoreType.DMA((len(operands),)),
            pltpu.VMEM((rows * residues // 2, 2 * channels), F32),
            pltpu.VMEM((rows * residues // 2 // LANES, 2 * hidden, LANES), F32),
            pltpu.VMEM((rows // hidden, pairs * hidden // LANES, LANES), F32),
            pltpu.VMEM((pairs // 2, hidden * hidden), BF16),
        ],
        compiler_params=pltpu.CompilerParams(vmem_limit_bytes=VMEM_LIMIT),
        name="outer_products",
    )(*(pltpu.with_memory_space_constraint(operand, pltpu.HBM) for operand in operands))
    kept = (left, right, coupling, counts)
    keep_here, keep_away = pl.pallas_call(
        outer_second_kernel,
        out_shape=[inside((pairs // 4, pair_channels), F32)] * 2,
        in_specs=[pl.BlockSpec(memory_space=pltpu.VMEM)] * len(kept),
        out_specs=[pl.BlockSpec(memory_space=pltpu.VMEM)] * 2,
        scratch_shapes=[pltpu.VMEM((pairs // 2, hidden * hidden), BF16)],
        compiler_params=pltpu.CompilerParams(vmem_limit_bytes=VMEM_LIMIT),
        cost_estimate=pl.CostEstimate(flops=1_000_000_000, bytes_accessed=2_000_000, transcendentals=0),
        name="outer_second",
    )(*(pltpu.with_memory_space_constraint(a, pltpu.VMEM) for a in kept))
    if relative:
        got_here = swap(send_here, size, 1)
        got_away, keep_away = lax.optimization_barrier((swap(send_away, size, 1), keep_away))
        away = (keep_away + got_away).reshape(4, own, pair_channels)
        far_away, features = lax.optimization_barrier((away[:2], features))
        far = swap(far_away, size, 2 + UNLIKE)
        first = transition(features, weights, 0, rows // 2)
        near_away, first = lax.optimization_barrier((away[2:], first))
        near = swap(near_away, size, 2 + UNLIKE)
        here = (keep_here + got_here).reshape(4, own, pair_channels)
        upper = here[:2] + far
        two, three = hop(upper[0], size, FIRST_HOP), hop(upper[1], size, SECOND_HOP)
        lower = here[2:] + near
        one = hop(lower[1], size, LAST_HOP)
        refreshed = transition(features, weights, rows // 2, rows - rows // 2, (first,))
        summands = (three, two, one, lower[0])
        pair_mean_update = pl.pallas_call(
            functools.partial(finish_kernel, residues),
            out_shape=jax.ShapeDtypeStruct((own, pair_channels), F32),
            in_specs=[pl.BlockSpec(memory_space=pltpu.VMEM)] * (len(summands) + 1),
            compiler_params=pltpu.CompilerParams(vmem_limit_bytes=VMEM_LIMIT),
            name="finish",
        )(*(pltpu.with_memory_space_constraint(a, pltpu.VMEM) for a in summands + (offset,)))
    else:
        refreshed = transition(features, weights, 0, rows)
        grid = jnp.concatenate([keep_here, keep_away, send_here, send_away], axis=0)
        grid = grid.reshape(residues, residues, pair_channels)
        counted = lax.psum(grid[:, residues - 1, :residues], "rows").reshape(size, own)
        counted = pick(counted, lax.axis_index("rows"), 0)[:, None]
        last = iota(grid.shape, 1) == residues - 1
        summed = scatter_sum(jnp.where(last, 0.0, grid).reshape(size, own, pair_channels), size)
        pair_mean_update = summed / jnp.maximum(counted, 1.0) + coupling_offset
    return pair_mean_update, refreshed


def solution(mesh):
    in_specs = (
        P(("groups", "rows"), None, None),
        P(("groups", "rows"), None),
        P("groups"),
    ) + (P(),) * 11
    out_specs = (P(("groups", "rows"), None), P(("groups", "rows"), None, None))
    return jax.shard_map(
        functools.partial(body, size=mesh.shape["rows"]),
        mesh=mesh, in_specs=in_specs, out_specs=out_specs, check_vma=False,
    )
```

```python
import functools

import jax
import jax.numpy as jnp
from jax import lax
from jax.experimental import pallas as pl
from jax.experimental.pallas import tpu as pltpu
from jax.sharding import PartitionSpec as P

F32 = jnp.float32
BF16 = jnp.bfloat16
EPS = 1e-05
LANES = 128
VMEM_LIMIT = 48 * 1024 * 1024
STEP = 16
JOIN = 4
CHUNK = 256
FIRST_HOP = (2, 3, 1, 0)
SECOND_HOP = (3, 2, 0, 1)
LAST_HOP = (1, 0, 3, 2)
TURNED = 0b0001
UNLIKE = 1
OWNERS = 16


def dot(a, b, dims=((1,), (0,))):
    return lax.dot_general(a, b, (dims, ((), ())), preferred_element_type=F32)


def two_halves(array, half):
    return jnp.concatenate([array[:, :half, :], array[:, half:, :]], axis=-1)


def twice(vector):
    return jnp.concatenate([vector, vector], axis=-1)


def block_pair(matrix):
    zero = jnp.zeros_like(matrix)
    return jnp.concatenate(
        [jnp.concatenate([matrix, zero], axis=1), jnp.concatenate([zero, matrix], axis=1)], axis=0
    )


def iota(shape, axis):
    return lax.broadcasted_iota(jnp.int32, shape, axis)


def mean_matrix(channels):
    shape = (2 * channels, 2 * channels)
    same = iota(shape, 0) // channels == iota(shape, 1) // channels
    return jnp.where(same, 1.0 / channels, 0.0).astype(BF16)


def standardize_pairs(values, averaging, gain, bias):
    centered = values.astype(F32) - dot(values, averaging)
    variance = dot((centered * centered).astype(BF16), averaging)
    return centered * lax.rsqrt(variance + EPS) * gain + bias


def ranks_along_z():
    table = 0
    for z, order in enumerate(zip(FIRST_HOP, SECOND_HOP, range(len(FIRST_HOP)), LAST_HOP)):
        for place_of, other in enumerate(order):
            table |= place_of << (z * 8 + (z ^ other) * 2)
    return table - (1 << 32) if table >> 31 else table


RANKS = ranks_along_z()


def relabel(device):
    return device ^ ((TURNED >> (device >> 2)) & 1)


def place(residue, me, per_owner):
    if me is None:
        return residue
    apart = relabel(residue // per_owner) ^ relabel(me)
    along_y = (apart >> 1) & 1
    along_z = (RANKS >> ((me >> 2) * 8 + (apart >> 2) * 2)) & 3
    rank = (((apart & 1) ^ (along_y & UNLIKE)) * 2 + along_y) * 4 + along_z
    return rank * per_owner + residue % per_owner


def outer_half(left, right, coupling, counts, x_mat, *out_refs):
    count = counts.shape[0]
    part = count // len(out_refs)
    residues = out_refs[0].shape[0] // part
    half = residues // 2
    groups = left.shape[0] // count
    rows = right.shape[0] // half
    quad = left.shape[1] // rows
    lane_group = iota((rows, LANES), 1) // (LANES // quad)
    masks = [lane_group == h4 for h4 in range(quad)]
    zero = jnp.zeros((rows, LANES), BF16)
    for j in range(0, residues, JOIN):
        beside = []
        for one_j in range(j, j + JOIN):
            side, p = one_j // half, one_j % half
            one = right[p * rows : (p + 1) * rows, side * LANES : (side + 1) * LANES]
            beside.append(jnp.concatenate([jnp.where(m, one, zero) for m in masks], axis=0))
        product = dot(left, jnp.concatenate(beside, axis=1)).astype(BF16)
        for n in range(JOIN):
            for g in range(groups):
                x_mat[(j + n) * count : (j + n + 1) * count, g * LANES : (g + 1) * LANES] = product[
                    g * count : (g + 1) * count, n * LANES : (n + 1) * LANES
                ]
    projected = [
        dot(x_mat[at : at + CHUNK, :], coupling) for at in range(0, residues * count, CHUNK)
    ]
    projected = jnp.concatenate(projected, axis=0)
    for j in range(residues):
        rows_j = counts if j == residues - 1 else projected[j * count : (j + 1) * count, :]
        for n, out_ref in enumerate(out_refs):
            out_ref[pl.ds(j, part, stride=residues), :] = rows_j[n * part : (n + 1) * part]


def outer_second_kernel(left_ref, right_ref, coupling_ref, counts_ref, here_ref, away_ref, x_mat):
    outer_half(left_ref[...], right_ref, coupling_ref[...], counts_ref[...], x_mat, here_ref, away_ref)


def outer_kernel(relative, n_inputs, n_handed, *refs):
    sources = refs[:n_inputs]
    outs, refs = refs[n_inputs : n_inputs + 5], refs[n_inputs + 5 :]
    here_ref, away_ref, left_ref, right_ref, counts_ref = outs
    handed = refs[:n_handed]
    own = n_inputs - n_handed
    early = own + 2
    targets = refs[n_handed : n_handed + own]
    arrived, x_scratch, left_t_scratch, left_scratch, x_mat = refs[n_handed + own :]
    presence_ref, position_ref, gain_ref, bias_ref, first_ref, second_ref = targets
    x_ref, coupling_ref = handed[:2]
    me = lax.axis_index("rows") if relative else None
    order = (handed[0],) + tuple(targets) + tuple(handed[1:])
    copies = [
        pltpu.make_async_copy(source, target, arrived.at[n])
        for n, (source, target) in enumerate(zip(sources, order))
    ]
    for copy in copies[:early]:
        copy.start()
    rows, residues, channels = x_ref.shape
    hidden = first_ref.shape[0]
    half = residues // 2
    per_owner = residues // OWNERS
    quad = LANES // hidden
    groups = hidden // quad
    square = (residues, residues)

    averaging = mean_matrix(channels)
    lanes = iota((residues, half * 2 * channels), 1)
    wanted = lanes // (2 * channels) + half * ((lanes % (2 * channels)) // channels)
    spread = jnp.where(iota(lanes.shape, 0) == wanted, 1.0, 0.0).astype(BF16)
    diagonal = iota(square, 0) == iota(square, 1)
    order = (place(iota(square, 1), me, per_owner) == iota(square, 0)).astype(BF16)

    for copy in copies[early:]:
        copy.start()
    for copy in copies[:early]:
        copy.wait()
    x_scratch[...] = two_halves(x_ref[...], half).astype(F32).reshape(rows * half, 2 * channels)
    tokens = jnp.concatenate(
        [x_scratch[pl.ds(p, rows, stride=half), :] for p in range(half)], axis=0
    ).astype(BF16)
    normed = standardize_pairs(tokens, averaging, twice(gain_ref[...]), twice(bias_ref[...]))

    position = jnp.where(diagonal, position_ref[...].astype(F32), 0.0).sum(axis=1, keepdims=True)
    valid = (presence_ref[...].astype(F32) * position).astype(BF16)
    flags = dot(valid, spread, ((0,), (0,)))
    flags = jnp.concatenate(
        [flags[:, p * 2 * channels : (p + 1) * 2 * channels] for p in range(half)], axis=0
    )
    normed = (normed * flags).astype(BF16)

    left_t = dot(block_pair(first_ref[...]), normed, ((1,), (1,)))
    for v in range(left_t_scratch.shape[0]):
        left_t_scratch[v] = left_t[:, v * LANES : (v + 1) * LANES]
    low = iota((groups, LANES), 1) < rows
    per = LANES // rows
    for side in range(2):
        for v in range(half // per):
            pieces = [
                left_t_scratch[v, pl.ds(side * hidden + h4, groups, stride=quad), :]
                for h4 in range(quad)
            ]
            turned = [pltpu.roll(piece, rows, 1) for piece in pieces]
            for odd in range(2):
                row = place(side * half + v * per + odd, me, per_owner)
                for c in range(quad // 2):
                    if odd:
                        tile = jnp.where(low, turned[2 * c], pieces[2 * c + 1])
                    else:
                        tile = jnp.where(low, pieces[2 * c], turned[2 * c + 1])
                    at = (row // half) * (groups * half) + row % half
                    left_scratch[c, pl.ds(at, groups, stride=half), :] = tile
    left = jnp.concatenate(
        [left_scratch[c] for c in range(quad // 2)], axis=1
    ).astype(BF16)

    repeated = jnp.concatenate([second_ref[...]] * quad, axis=0)
    right = dot(normed, block_pair(repeated), ((1,), (1,))).astype(BF16)
    right_ref[...] = right
    left_ref[...] = left[: groups * half]
    counts = dot(dot(order, valid).astype(BF16), valid, ((1,), (1,)))
    counts = jnp.concatenate([counts, jnp.zeros((residues, LANES - residues), F32)], axis=1)
    counts_ref[...] = counts[:half]
    outer_half(left[groups * half :], right, coupling_ref[...], counts[half:], x_mat, here_ref, away_ref)
    for copy in copies[early:]:
        copy.wait()


def transition_rows(x_ref, start, count, gain_ref, bias_ref, switch_ref, expand_ref, contract_ref, out_ref):
    _, residues, channels = x_ref.shape
    half = residues // 2
    averaging = mean_matrix(channels)
    gain, bias = twice(gain_ref[...]), twice(bias_ref[...])
    switch = block_pair(switch_ref[...])
    expand = block_pair(expand_ref[...])
    contract = block_pair(contract_ref[...])
    for at in range(0, count, STEP):
        pairs = two_halves(x_ref[start + at : start + at + STEP], half).reshape(STEP * half, 2 * channels)
        normed = standardize_pairs(pairs, averaging, gain, bias).astype(BF16)
        gate = dot(normed, switch) * 0.5
        inner = ((gate + gate * jnp.tanh(gate)) * dot(normed, expand)).astype(BF16)
        result = (pairs.astype(F32) + dot(inner, contract, ((1,), (1,)))).astype(BF16)
        result = result.reshape(STEP, half, 2 * channels)
        out_ref[at : at + STEP, :half, :] = result[:, :, :channels]
        out_ref[at : at + STEP, half:, :] = result[:, :, channels:]
        yield at


def transition_part(start, x_ref, *refs):
    *weight_refs, out_ref = refs
    for _ in transition_rows(x_ref, start, out_ref.shape[0], *weight_refs, out_ref):
        pass


def transition_last(n_parts, x_ref, *refs):
    weight_refs = refs[: -3 - n_parts]
    part_refs = refs[-3 - n_parts : -3]
    out_hbm, result_ref, sent = refs[-3:]
    copies = []

    def send(source, at, count):
        copies.append(pltpu.make_async_copy(source, out_hbm.at[pl.ds(at, count)], sent.at[len(copies)]))
        copies[-1].start()

    head = 0
    for part_ref in part_refs:
        send(part_ref, head, part_ref.shape[0])
        head += part_ref.shape[0]
    for at in transition_rows(x_ref, head, result_ref.shape[0], *weight_refs, result_ref):
        send(result_ref.at[pl.ds(at, STEP)], head + at, STEP)
    for copy in copies:
        copy.wait()


def finish_kernel(residues, *refs):
    *summand_refs, offset_ref, out_ref = refs
    total = summand_refs[0][...]
    for ref in summand_refs[1:]:
        total = total + ref[...]
    square = (residues, residues)
    diagonal = iota(square, 0) == iota(square, 1)
    last = iota((residues, total.shape[1]), 0) == residues - 1
    for start in range(0, total.shape[0], residues):
        block = total[start : start + residues]
        counts = jnp.where(diagonal, block[residues - 1 :, :residues], 0.0).sum(axis=1, keepdims=True)
        mean = jnp.where(last, 0.0, block) / jnp.maximum(counts, 1.0)
        out_ref[start : start + residues, :] = mean + offset_ref[...]


def pick(array, index, axis):
    return lax.dynamic_index_in_dim(array, index, axis, keepdims=False)


def swap(array, size, apart):
    return lax.ppermute(array, "rows", [(i, i ^ apart) for i in range(size)])


def hop(array, size, targets):
    step = size // len(targets)
    pairs = [(i, relabel(targets[i // step] * step + relabel(i) % step)) for i in range(size)]
    return lax.ppermute(array, "rows", pairs)


def scatter_sum(partial, size):
    me = lax.axis_index("rows")
    tail = partial.shape[1:]
    done = 1
    while size // done > 4 or (size // done) % 4:
        parts = partial.reshape((size // done // 2, 2) + tail)
        mine = (me // done) % 2
        partial = pick(parts, mine, 1) + swap(pick(parts, 1 - mine, 1), size, done)
        done *= 2
    mine = me // done
    total = pick(partial, mine, 0)
    for k in range(1, size // done):
        total = total + swap(pick(partial, mine ^ k, 0), size, k * done)
    return total


def inside(shape, dtype):
    return pltpu.VMEM(shape, dtype)


def transition(features, weights, start, count, parts=()):
    rows, residues, channels = features.shape
    operands = [features, *weights, *parts]
    last = start + count == rows
    return pl.pallas_call(
        functools.partial(transition_last, len(parts)) if last else functools.partial(transition_part, start),
        out_shape=jax.ShapeDtypeStruct(features.shape, BF16) if last else inside((count, residues, channels), BF16),
        in_specs=[pl.BlockSpec(memory_space=pltpu.VMEM)] * len(operands),
        out_specs=pl.BlockSpec(memory_space=pltpu.HBM if last else pltpu.VMEM),
        scratch_shapes=[
            pltpu.VMEM((count, residues, channels), BF16),
            pltpu.SemaphoreType.DMA((len(parts) + count // STEP,)),
        ] if last else [],
        compiler_params=pltpu.CompilerParams(vmem_limit_bytes=VMEM_LIMIT),
        cost_estimate=pl.CostEstimate(
            flops=6_000_000 * count, bytes_accessed=30_000 * count, transcendentals=8_000 * count
        ),
        name="transition_last" if last else "transition_part",
    )(*(pltpu.with_memory_space_constraint(a, pltpu.VMEM) for a in operands))


def body(
    sequence_features,
    sequence_presence,
    position_presence,
    product_scale_vector,
    product_shift_vector,
    first_factor_matrix,
    second_factor_matrix,
    coupling_matrix,
    coupling_offset,
    feedforward_scale_vector,
    feedforward_shift_vector,
    feedforward_switch_matrix,
    feedforward_expand_matrix,
    feedforward_contract_matrix,
    *,
    size,
):
    rows, residues, channels = sequence_features.shape
    hidden = first_factor_matrix.shape[1]
    pair_channels = coupling_matrix.shape[1]
    pairs = residues * residues
    own = pairs // size
    relative = size == OWNERS
    row = lambda v: v.reshape(1, -1)
    used = (
        sequence_presence.T,
        row(position_presence),
        row(product_scale_vector),
        row(product_shift_vector),
        first_factor_matrix.T,
        second_factor_matrix.T,
    )
    handed = (
        sequence_features,
        coupling_matrix,
        row(coupling_offset),
        row(feedforward_scale_vector),
        row(feedforward_shift_vector),
        feedforward_switch_matrix,
        feedforward_expand_matrix,
        feedforward_contract_matrix.T,
    )
    operands = handed[:1] + used + handed[1:]
    split = (pairs * hidden // LANES // 2, rows * LANES // hidden)
    results = [
        inside((pairs // 4, pair_channels), F32),
        inside((pairs // 4, pair_channels), F32),
        inside(split, BF16),
        inside((rows * residues // 2, 2 * LANES), BF16),
        inside((residues // 2, LANES), F32),
    ]
    results += [inside(operand.shape, operand.dtype) for operand in handed]
    send_here, send_away, left, right, counts, features, coupling, offset, *weights = pl.pallas_call(
        functools.partial(outer_kernel, relative, len(operands), len(handed)),
        out_shape=results,
        in_specs=[pl.BlockSpec(memory_space=pltpu.HBM)] * len(operands),
        out_specs=[pl.BlockSpec(memory_space=pltpu.VMEM)] * len(results),
        scratch_shapes=[pltpu.VMEM(operand.shape, operand.dtype) for operand in used] + [
            pltpu.SemaphoreType.DMA((len(operands),)),
            pltpu.VMEM((rows * residues // 2, 2 * channels), F32),
            pltpu.VMEM((rows * residues // 2 // LANES, 2 * hidden, LANES), F32),
            pltpu.VMEM((rows // hidden, pairs * hidden // LANES, LANES), F32),
            pltpu.VMEM((pairs // 2, hidden * hidden), BF16),
        ],
        compiler_params=pltpu.CompilerParams(vmem_limit_bytes=VMEM_LIMIT),
        name="outer_products",
    )(*(pltpu.with_memory_space_constraint(operand, pltpu.HBM) for operand in operands))
    kept = (left, right, coupling, counts)
    keep_here, keep_away = pl.pallas_call(
        outer_second_kernel,
        out_shape=[inside((pairs // 4, pair_channels), F32)] * 2,
        in_specs=[pl.BlockSpec(memory_space=pltpu.VMEM)] * len(kept),
        out_specs=[pl.BlockSpec(memory_space=pltpu.VMEM)] * 2,
        scratch_shapes=[pltpu.VMEM((pairs // 2, hidden * hidden), BF16)],
        compiler_params=pltpu.CompilerParams(vmem_limit_bytes=VMEM_LIMIT),
        cost_estimate=pl.CostEstimate(flops=1_000_000_000, bytes_accessed=2_000_000, transcendentals=0),
        name="outer_second",
    )(*(pltpu.with_memory_space_constraint(a, pltpu.VMEM) for a in kept))
    if relative:
        got_here = swap(send_here, size, 1)
        got_away, keep_away = lax.optimization_barrier((swap(send_away, size, 1), keep_away))
        away = (keep_away + got_away).reshape(4, own, pair_channels)
        far_away, features = lax.optimization_barrier((away[:2], features))
        far = swap(far_away, size, 2 + UNLIKE)
        first = transition(features, weights, 0, rows // 2)
        near_away, first = lax.optimization_barrier((away[2:], first))
        near = swap(near_away, size, 2 + UNLIKE)
        here = (keep_here + got_here).reshape(4, own, pair_channels)
        upper = here[:2] + far
        two, three = hop(upper[0], size, FIRST_HOP), hop(upper[1], size, SECOND_HOP)
        lower = here[2:] + near
        one = hop(lower[1], size, LAST_HOP)
        refreshed = transition(features, weights, rows // 2, rows - rows // 2, (first,))
        summands = (three, two, one, lower[0])
        pair_mean_update = pl.pallas_call(
            functools.partial(finish_kernel, residues),
            out_shape=jax.ShapeDtypeStruct((own, pair_channels), F32),
            in_specs=[pl.BlockSpec(memory_space=pltpu.VMEM)] * (len(summands) + 1),
            compiler_params=pltpu.CompilerParams(vmem_limit_bytes=VMEM_LIMIT),
            name="finish",
        )(*(pltpu.with_memory_space_constraint(a, pltpu.VMEM) for a in summands + (offset,)))
    else:
        refreshed = transition(features, weights, 0, rows)
        grid = jnp.concatenate([keep_here, keep_away, send_here, send_away], axis=0)
        grid = grid.reshape(residues, residues, pair_channels)
        counted = lax.psum(grid[:, residues - 1, :residues], "rows").reshape(size, own)
        counted = pick(counted, lax.axis_index("rows"), 0)[:, None]
        last = iota(grid.shape, 1) == residues - 1
        summed = scatter_sum(jnp.where(last, 0.0, grid).reshape(size, own, pair_channels), size)
        pair_mean_update = summed / jnp.maximum(counted, 1.0) + coupling_offset
    return pair_mean_update, refreshed


def solution(mesh):
    in_specs = (
        P(("groups", "rows"), None, None),
        P(("groups", "rows"), None),
        P("groups"),
    ) + (P(),) * 11
    out_specs = (P(("groups", "rows"), None), P(("groups", "rows"), None, None))
    return jax.shard_map(
        functools.partial(body, size=mesh.shape["rows"]),
        mesh=mesh, in_specs=in_specs, out_specs=out_specs, check_vma=False,
    )
```

```python
import functools

import jax
import jax.numpy as jnp
from jax import lax
from jax.experimental import pallas as pl
from jax.experimental.pallas import tpu as pltpu
from jax.sharding import PartitionSpec as P

F32 = jnp.float32
BF16 = jnp.bfloat16
EPS = 1e-05
LANES = 128
VMEM_LIMIT = 48 * 1024 * 1024
STEP = 16
JOIN = 4
CHUNK = 256
FIRST_HOP = (2, 3, 1, 0)
SECOND_HOP = (3, 2, 0, 1)
LAST_HOP = (1, 0, 3, 2)
TURNED = 0b0001
UNLIKE = 1
OWNERS = 16


def dot(a, b, dims=((1,), (0,))):
    return lax.dot_general(a, b, (dims, ((), ())), preferred_element_type=F32)


def two_halves(array, half):
    return jnp.concatenate([array[:, :half, :], array[:, half:, :]], axis=-1)


def twice(vector):
    return jnp.concatenate([vector, vector], axis=-1)


def block_pair(matrix):
    zero = jnp.zeros_like(matrix)
    return jnp.concatenate(
        [jnp.concatenate([matrix, zero], axis=1), jnp.concatenate([zero, matrix], axis=1)], axis=0
    )


def iota(shape, axis):
    return lax.broadcasted_iota(jnp.int32, shape, axis)


def mean_matrix(channels):
    shape = (2 * channels, 2 * channels)
    same = iota(shape, 0) // channels == iota(shape, 1) // channels
    return jnp.where(same, 1.0 / channels, 0.0).astype(BF16)


def standardize_pairs(values, averaging, gain, bias):
    centered = values.astype(F32) - dot(values, averaging)
    variance = dot((centered * centered).astype(BF16), averaging)
    return centered * lax.rsqrt(variance + EPS) * gain + bias


def ranks_along_z():
    table = 0
    for z, order in enumerate(zip(FIRST_HOP, SECOND_HOP, range(len(FIRST_HOP)), LAST_HOP)):
        for place_of, other in enumerate(order):
            table |= place_of << (z * 8 + (z ^ other) * 2)
    return table - (1 << 32) if table >> 31 else table


RANKS = ranks_along_z()


def relabel(device):
    return device ^ ((TURNED >> (device >> 2)) & 1)


def place(residue, me, per_owner):
    if me is None:
        return residue
    apart = relabel(residue // per_owner) ^ relabel(me)
    along_y = (apart >> 1) & 1
    along_z = (RANKS >> ((me >> 2) * 8 + (apart >> 2) * 2)) & 3
    rank = (((apart & 1) ^ (along_y & UNLIKE)) * 2 + along_y) * 4 + along_z
    return rank * per_owner + residue % per_owner


def outer_half(left, right, coupling, counts, x_mat, *out_refs):
    count = counts.shape[0]
    part = count // len(out_refs)
    residues = out_refs[0].shape[0] // part
    half = residues // 2
    groups = left.shape[0] // count
    rows = right.shape[0] // half
    quad = left.shape[1] // rows
    lane_group = iota((rows, LANES), 1) // (LANES // quad)
    masks = [lane_group == h4 for h4 in range(quad)]
    zero = jnp.zeros((rows, LANES), BF16)
    for j in range(0, residues, JOIN):
        beside = []
        for one_j in range(j, j + JOIN):
            side, p = one_j // half, one_j % half
            one = right[p * rows : (p + 1) * rows, side * LANES : (side + 1) * LANES]
            beside.append(jnp.concatenate([jnp.where(m, one, zero) for m in masks], axis=0))
        product = dot(left, jnp.concatenate(beside, axis=1)).astype(BF16)
        for n in range(JOIN):
            for g in range(groups):
                x_mat[(j + n) * count : (j + n + 1) * count, g * LANES : (g + 1) * LANES] = product[
                    g * count : (g + 1) * count, n * LANES : (n + 1) * LANES
                ]
    projected = [
        dot(x_mat[at : at + CHUNK, :], coupling) for at in range(0, residues * count, CHUNK)
    ]
    projected = jnp.concatenate(projected, axis=0)
    for j in range(residues):
        rows_j = counts if j == residues - 1 else projected[j * count : (j + 1) * count, :]
        for n, out_ref in enumerate(out_refs):
            out_ref[pl.ds(j, part, stride=residues), :] = rows_j[n * part : (n + 1) * part]


def outer_second_kernel(left_ref, right_ref, coupling_ref, counts_ref, here_ref, away_ref, x_mat):
    outer_half(left_ref[...], right_ref, coupling_ref[...], counts_ref[...], x_mat, here_ref, away_ref)


def outer_kernel(relative, n_inputs, n_handed, *refs):
    sources = refs[:n_inputs]
    outs, refs = refs[n_inputs : n_inputs + 5], refs[n_inputs + 5 :]
    here_ref, away_ref, left_ref, right_ref, counts_ref = outs
    handed = refs[:n_handed]
    own = n_inputs - n_handed
    early = own + 2
    targets = refs[n_handed : n_handed + own]
    arrived, x_scratch, left_t_scratch, left_scratch, x_mat = refs[n_handed + own :]
    presence_ref, position_ref, gain_ref, bias_ref, first_ref, second_ref = targets
    x_ref, coupling_ref = handed[:2]
    me = lax.axis_index("rows") if relative else None
    order = (handed[0],) + tuple(targets) + tuple(handed[1:])
    copies = [
        pltpu.make_async_copy(source, target, arrived.at[n])
        for n, (source, target) in enumerate(zip(sources, order))
    ]
    for copy in copies[:early]:
        copy.start()
    rows, residues, channels = x_ref.shape
    hidden = first_ref.shape[0]
    half = residues // 2
    per_owner = residues // OWNERS
    quad = LANES // hidden
    groups = hidden // quad
    square = (residues, residues)

    averaging = mean_matrix(channels)
    lanes = iota((residues, half * 2 * channels), 1)
    wanted = lanes // (2 * channels) + half * ((lanes % (2 * channels)) // channels)
    spread = jnp.where(iota(lanes.shape, 0) == wanted, 1.0, 0.0).astype(BF16)
    diagonal = iota(square, 0) == iota(square, 1)
    order = (place(iota(square, 1), me, per_owner) == iota(square, 0)).astype(BF16)

    for copy in copies[early:]:
        copy.start()
    for copy in copies[:early]:
        copy.wait()
    x_scratch[...] = two_halves(x_ref[...], half).astype(F32).reshape(rows * half, 2 * channels)
    tokens = jnp.concatenate(
        [x_scratch[pl.ds(p, rows, stride=half), :] for p in range(half)], axis=0
    ).astype(BF16)
    normed = standardize_pairs(tokens, averaging, twice(gain_ref[...]), twice(bias_ref[...]))

    position = jnp.where(diagonal, position_ref[...].astype(F32), 0.0).sum(axis=1, keepdims=True)
    valid = (presence_ref[...].astype(F32) * position).astype(BF16)
    flags = dot(valid, spread, ((0,), (0,)))
    counts = dot(dot(order, valid).astype(BF16), valid, ((1,), (1,)))
    counts = jnp.concatenate([counts, jnp.zeros((residues, LANES - residues), F32)], axis=1)
    counts_ref[...] = counts[:half]
    flags = jnp.concatenate(
        [flags[:, p * 2 * channels : (p + 1) * 2 * channels] for p in range(half)], axis=0
    )
    normed = (normed * flags).astype(BF16)

    left_t = dot(block_pair(first_ref[...]), normed, ((1,), (1,)))
    for v in range(left_t_scratch.shape[0]):
        left_t_scratch[v] = left_t[:, v * LANES : (v + 1) * LANES]
    low = iota((groups, LANES), 1) < rows
    per = LANES // rows
    for side in range(2):
        for v in range(half // per):
            pieces = [
                left_t_scratch[v, pl.ds(side * hidden + h4, groups, stride=quad), :]
                for h4 in range(quad)
            ]
            turned = [pltpu.roll(piece, rows, 1) for piece in pieces]
            for odd in range(2):
                row = place(side * half + v * per + odd, me, per_owner)
                for c in range(quad // 2):
                    if odd:
                        tile = jnp.where(low, turned[2 * c], pieces[2 * c + 1])
                    else:
                        tile = jnp.where(low, pieces[2 * c], turned[2 * c + 1])
                    at = (row // half) * (groups * half) + row % half
                    left_scratch[c, pl.ds(at, groups, stride=half), :] = tile
    left = jnp.concatenate(
        [left_scratch[c] for c in range(quad // 2)], axis=1
    ).astype(BF16)

    repeated = jnp.concatenate([second_ref[...]] * quad, axis=0)
    right = dot(normed, block_pair(repeated), ((1,), (1,))).astype(BF16)
    right_ref[...] = right
    left_ref[...] = left[: groups * half]
    outer_half(left[groups * half :], right, coupling_ref[...], counts[half:], x_mat, here_ref, away_ref)
    for copy in copies[early:]:
        copy.wait()


def transition_rows(x_ref, start, count, gain_ref, bias_ref, switch_ref, expand_ref, contract_ref, out_ref):
    _, residues, channels = x_ref.shape
    half = residues // 2
    averaging = mean_matrix(channels)
    gain, bias = twice(gain_ref[...]), twice(bias_ref[...])
    switch = block_pair(switch_ref[...])
    expand = block_pair(expand_ref[...])
    contract = block_pair(contract_ref[...])
    for at in range(0, count, STEP):
        pairs = two_halves(x_ref[start + at : start + at + STEP], half).reshape(STEP * half, 2 * channels)
        normed = standardize_pairs(pairs, averaging, gain, bias).astype(BF16)
        gate = dot(normed, switch) * 0.5
        inner = ((gate + gate * jnp.tanh(gate)) * dot(normed, expand)).astype(BF16)
        result = (pairs.astype(F32) + dot(inner, contract, ((1,), (1,)))).astype(BF16)
        result = result.reshape(STEP, half, 2 * channels)
        out_ref[at : at + STEP, :half, :] = result[:, :, :channels]
        out_ref[at : at + STEP, half:, :] = result[:, :, channels:]
        yield at


def transition_part(start, x_ref, *refs):
    *weight_refs, out_ref = refs
    for _ in transition_rows(x_ref, start, out_ref.shape[0], *weight_refs, out_ref):
        pass


def transition_last(n_parts, x_ref, *refs):
    weight_refs = refs[: -3 - n_parts]
    part_refs = refs[-3 - n_parts : -3]
    out_hbm, result_ref, sent = refs[-3:]
    copies = []

    def send(source, at, count):
        copies.append(pltpu.make_async_copy(source, out_hbm.at[pl.ds(at, count)], sent.at[len(copies)]))
        copies[-1].start()

    head = 0
    for part_ref in part_refs:
        send(part_ref, head, part_ref.shape[0])
        head += part_ref.shape[0]
    for at in transition_rows(x_ref, head, result_ref.shape[0], *weight_refs, result_ref):
        send(result_ref.at[pl.ds(at, STEP)], head + at, STEP)
    for copy in copies:
        copy.wait()


def finish_kernel(residues, *refs):
    *summand_refs, offset_ref, out_ref = refs
    total = summand_refs[0][...]
    for ref in summand_refs[1:]:
        total = total + ref[...]
    square = (residues, residues)
    diagonal = iota(square, 0) == iota(square, 1)
    last = iota((residues, total.shape[1]), 0) == residues - 1
    for start in range(0, total.shape[0], residues):
        block = total[start : start + residues]
        counts = jnp.where(diagonal, block[residues - 1 :, :residues], 0.0).sum(axis=1, keepdims=True)
        mean = jnp.where(last, 0.0, block) / jnp.maximum(counts, 1.0)
        out_ref[start : start + residues, :] = mean + offset_ref[...]


def pick(array, index, axis):
    return lax.dynamic_index_in_dim(array, index, axis, keepdims=False)


def swap(array, size, apart):
    return lax.ppermute(array, "rows", [(i, i ^ apart) for i in range(size)])


def hop(array, size, targets):
    step = size // len(targets)
    pairs = [(i, relabel(targets[i // step] * step + relabel(i) % step)) for i in range(size)]
    return lax.ppermute(array, "rows", pairs)


def scatter_sum(partial, size):
    me = lax.axis_index("rows")
    tail = partial.shape[1:]
    done = 1
    while size // done > 4 or (size // done) % 4:
        parts = partial.reshape((size // done // 2, 2) + tail)
        mine = (me // done) % 2
        partial = pick(parts, mine, 1) + swap(pick(parts, 1 - mine, 1), size, done)
        done *= 2
    mine = me // done
    total = pick(partial, mine, 0)
    for k in range(1, size // done):
        total = total + swap(pick(partial, mine ^ k, 0), size, k * done)
    return total


def inside(shape, dtype):
    return pltpu.VMEM(shape, dtype)


def transition(features, weights, start, count, parts=()):
    rows, residues, channels = features.shape
    operands = [features, *weights, *parts]
    last = start + count == rows
    return pl.pallas_call(
        functools.partial(transition_last, len(parts)) if last else functools.partial(transition_part, start),
        out_shape=jax.ShapeDtypeStruct(features.shape, BF16) if last else inside((count, residues, channels), BF16),
        in_specs=[pl.BlockSpec(memory_space=pltpu.VMEM)] * len(operands),
        out_specs=pl.BlockSpec(memory_space=pltpu.HBM if last else pltpu.VMEM),
        scratch_shapes=[
            pltpu.VMEM((count, residues, channels), BF16),
            pltpu.SemaphoreType.DMA((len(parts) + count // STEP,)),
        ] if last else [],
        compiler_params=pltpu.CompilerParams(vmem_limit_bytes=VMEM_LIMIT),
        cost_estimate=pl.CostEstimate(
            flops=6_000_000 * count, bytes_accessed=30_000 * count, transcendentals=8_000 * count
        ),
        name="transition_last" if last else "transition_part",
    )(*(pltpu.with_memory_space_constraint(a, pltpu.VMEM) for a in operands))


def body(
    sequence_features,
    sequence_presence,
    position_presence,
    product_scale_vector,
    product_shift_vector,
    first_factor_matrix,
    second_factor_matrix,
    coupling_matrix,
    coupling_offset,
    feedforward_scale_vector,
    feedforward_shift_vector,
    feedforward_switch_matrix,
    feedforward_expand_matrix,
    feedforward_contract_matrix,
    *,
    size,
):
    rows, residues, channels = sequence_features.shape
    hidden = first_factor_matrix.shape[1]
    pair_channels = coupling_matrix.shape[1]
    pairs = residues * residues
    own = pairs // size
    relative = size == OWNERS
    row = lambda v: v.reshape(1, -1)
    used = (
        sequence_presence.T,
        row(position_presence),
        row(product_scale_vector),
        row(product_shift_vector),
        first_factor_matrix.T,
        second_factor_matrix.T,
    )
    handed = (
        sequence_features,
        coupling_matrix,
        row(coupling_offset),
        row(feedforward_scale_vector),
        row(feedforward_shift_vector),
        feedforward_switch_matrix,
        feedforward_expand_matrix,
        feedforward_contract_matrix.T,
    )
    operands = handed[:1] + used + handed[1:]
    split = (pairs * hidden // LANES // 2, rows * LANES // hidden)
    results = [
        inside((pairs // 4, pair_channels), F32),
        inside((pairs // 4, pair_channels), F32),
        inside(split, BF16),
        inside((rows * residues // 2, 2 * LANES), BF16),
        inside((residues // 2, LANES), F32),
    ]
    results += [inside(operand.shape, operand.dtype) for operand in handed]
    send_here, send_away, left, right, counts, features, coupling, offset, *weights = pl.pallas_call(
        functools.partial(outer_kernel, relative, len(operands), len(handed)),
        out_shape=results,
        in_specs=[pl.BlockSpec(memory_space=pltpu.HBM)] * len(operands),
        out_specs=[pl.BlockSpec(memory_space=pltpu.VMEM)] * len(results),
        scratch_shapes=[pltpu.VMEM(operand.shape, operand.dtype) for operand in used] + [
            pltpu.SemaphoreType.DMA((len(operands),)),
            pltpu.VMEM((rows * residues // 2, 2 * channels), F32),
            pltpu.VMEM((rows * residues // 2 // LANES, 2 * hidden, LANES), F32),
            pltpu.VMEM((rows // hidden, pairs * hidden // LANES, LANES), F32),
            pltpu.VMEM((pairs // 2, hidden * hidden), BF16),
        ],
        compiler_params=pltpu.CompilerParams(vmem_limit_bytes=VMEM_LIMIT),
        name="outer_products",
    )(*(pltpu.with_memory_space_constraint(operand, pltpu.HBM) for operand in operands))
    kept = (left, right, coupling, counts)
    keep_here, keep_away = pl.pallas_call(
        outer_second_kernel,
        out_shape=[inside((pairs // 4, pair_channels), F32)] * 2,
        in_specs=[pl.BlockSpec(memory_space=pltpu.VMEM)] * len(kept),
        out_specs=[pl.BlockSpec(memory_space=pltpu.VMEM)] * 2,
        scratch_shapes=[pltpu.VMEM((pairs // 2, hidden * hidden), BF16)],
        compiler_params=pltpu.CompilerParams(vmem_limit_bytes=VMEM_LIMIT),
        cost_estimate=pl.CostEstimate(flops=1_000_000_000, bytes_accessed=2_000_000, transcendentals=0),
        name="outer_second",
    )(*(pltpu.with_memory_space_constraint(a, pltpu.VMEM) for a in kept))
    if relative:
        got_here = swap(send_here, size, 1)
        got_away, keep_away = lax.optimization_barrier((swap(send_away, size, 1), keep_away))
        away = (keep_away + got_away).reshape(4, own, pair_channels)
        far_away, features = lax.optimization_barrier((away[:2], features))
        far = swap(far_away, size, 2 + UNLIKE)
        first = transition(features, weights, 0, rows // 2)
        near_away, first = lax.optimization_barrier((away[2:], first))
        near = swap(near_away, size, 2 + UNLIKE)
        here = (keep_here + got_here).reshape(4, own, pair_channels)
        upper = here[:2] + far
        two, three = hop(upper[0], size, FIRST_HOP), hop(upper[1], size, SECOND_HOP)
        lower = here[2:] + near
        one = hop(lower[1], size, LAST_HOP)
        refreshed = transition(features, weights, rows // 2, rows - rows // 2, (first,))
        summands = (three, two, one, lower[0])
        pair_mean_update = pl.pallas_call(
            functools.partial(finish_kernel, residues),
            out_shape=jax.ShapeDtypeStruct((own, pair_channels), F32),
            in_specs=[pl.BlockSpec(memory_space=pltpu.VMEM)] * (len(summands) + 1),
            compiler_params=pltpu.CompilerParams(vmem_limit_bytes=VMEM_LIMIT),
            name="finish",
        )(*(pltpu.with_memory_space_constraint(a, pltpu.VMEM) for a in summands + (offset,)))
    else:
        refreshed = transition(features, weights, 0, rows)
        grid = jnp.concatenate([keep_here, keep_away, send_here, send_away], axis=0)
        grid = grid.reshape(residues, residues, pair_channels)
        counted = lax.psum(grid[:, residues - 1, :residues], "rows").reshape(size, own)
        counted = pick(counted, lax.axis_index("rows"), 0)[:, None]
        last = iota(grid.shape, 1) == residues - 1
        summed = scatter_sum(jnp.where(last, 0.0, grid).reshape(size, own, pair_channels), size)
        pair_mean_update = summed / jnp.maximum(counted, 1.0) + coupling_offset
    return pair_mean_update, refreshed


def solution(mesh):
    in_specs = (
        P(("groups", "rows"), None, None),
        P(("groups", "rows"), None),
        P("groups"),
    ) + (P(),) * 11
    out_specs = (P(("groups", "rows"), None), P(("groups", "rows"), None, None))
    return jax.shard_map(
        functools.partial(body, size=mesh.shape["rows"]),
        mesh=mesh, in_specs=in_specs, out_specs=out_specs, check_vma=False,
    )
```
